32 devices in a mesh: dp: 8 (over y, x, core), fsdp: 4 (over z).
Axes of the slice: x: 2, y: 2, z: 4, core: 2. Of those that a mesh axis runs over, the one named last changes fastest.
Arguments:
- tokens: float32 [32768, 1024], P(('dp', 'fsdp')), may hold values from -6 to 6
- w_query: float32 [1024, 1024], P(('dp', 'fsdp')), may hold values from -0.1875 to 0.1875
- w_key: float32 [1024, 1024], P(('dp', 'fsdp')), may hold values from -0.1875 to 0.1875
- w_value: float32 [1024, 1024], P(('dp', 'fsdp')), may hold values from -0.1875 to 0.1875
- w_output: float32 [1024, 1024], P(('dp', 'fsdp')), may hold values from -1.5 to 1.5
- gain_one: float32 [1024], P(('dp', 'fsdp')), may hold values from 0.1 to 1.9
- shift_one: float32 [1024], P(('dp', 'fsdp')), may hold values from -1.5 to 1.5
- gain_two: float32 [1024], P(('dp', 'fsdp')), may hold values from 0.1 to 1.9
- shift_two: float32 [1024], P(('dp', 'fsdp')), may hold values from -1.5 to 1.5
- expert_in: float32 [1024, 2, 4096], P(('dp', 'fsdp')), may hold values from -0.1875 to 0.1875
- expert_out: float32 [4096, 2, 1024], P(('dp', 'fsdp')), may hold values from -0.09375 to 0.09375
- lengths: int32 [32, 8], P(('dp', 'fsdp')), may hold values from 1 to 768, 1024 in all within a row
- expert_ids: int32 [32768, 1], P(('dp', 'fsdp')), may hold values from 0 to 1; in each aligned block of 1024 rows (0 to 1023, 1024 to 2047, ...) at most 640 rows name the same one
- padding: int32 [32768], P(('dp', 'fsdp')), may hold values 0 or 1
- cotangent: float32 [32768, 1024], P(('dp', 'fsdp')), may hold values from -6 to 6
Outputs:
- output: float32 [32768, 1024], P(('dp', 'fsdp'))
- grad_tokens: float32 [32768, 1024], P(('dp', 'fsdp'))
- grad_query: float32 [1024, 1024], P(('dp', 'fsdp'))
- grad_key: float32 [1024, 1024], P(('dp', 'fsdp'))
- grad_value: float32 [1024, 1024], P(('dp', 'fsdp'))
- grad_output: float32 [1024, 1024], P(('dp', 'fsdp'))
- grad_gain_one: float32 [1024], P(('dp', 'fsdp'))
- grad_shift_one: float32 [1024], P(('dp', 'fsdp'))
- grad_gain_two: float32 [1024], P(('dp', 'fsdp'))
- grad_shift_two: float32 [1024], P(('dp', 'fsdp'))
- grad_expert_in: float32 [1024, 2, 4096], P(('dp', 'fsdp'))
- grad_expert_out: float32 [4096, 2, 1024], P(('dp', 'fsdp'))
The draws below stay inside these ranges and needn't reach their ends.
Inputs may be any that keep to these rules, and one draw needn't show every extreme that they name: `expert_ids`: in each device's rows every expert is named at most 640 times, a bound that some block reaches. Each device's 8 lengths sum to 1024, and the longest is exactly 768.
All inputs are finite; a program needn't handle non-finite values. No bound on the sum of `padding` on one device may be relied on, other than what follows from the above.
Results may differ from the reference program's by a relative error of at most 0.01.
The reference program's roundings to bfloat16 on the way count: a program that leaves them out, or rounds other values in their place, can miss the bound.
Values may be sent and summed in bfloat16 or wider, within the bound.
No kernel may reach another device: no remote copies, remote signals or barrier semaphores. Data moves between devices by JAX's collectives and lax.ppermute only.
A program may use at most 512 MiB of HBM per device.

```python
import math
import jax
import jax.numpy as jnp
import numpy as np
from jax import lax

D = 1024
HEADS = 16
HEAD_DIM = 64
FFN = 4096
EXPERTS = 2
TOK_DEV = 1024
SEQ_DEV = 8
MAXLEN = 768
CAP = 640
TOKENS = 32768
DEVICES = 32


def with_ends(entries, key, least, largest):
    place = [jax.random.randint(jax.random.fold_in(key, axis), (), 0, length) for axis, length in enumerate(entries.shape)]
    main_axis = entries.shape.index(max(entries.shape))
    next_to = place[:main_axis] + [(place[main_axis] + 1) % entries.shape[main_axis]] + place[main_axis + 1:]
    return entries.at[tuple(place)].set(least).at[tuple(next_to)].set(largest)


def with_spikes(drawn, key, source, target, parts, factor):
    owner, partner = [(jnp.arange(drawn.shape[dim]) // (drawn.shape[dim] // parts)).reshape([-1 if axis == dim else 1 for axis in range(drawn.ndim)]) for dim in (source, target)]
    chosen = jax.random.permutation(key, parts)[partner]
    strong = (owner == chosen) | (owner == (partner + parts // 2) % parts)
    return jnp.where(strong, factor * drawn, drawn)


def steps_of(key, shape, cuts, smallest, largest):
    def one(dim, blocks):
        steps = jax.random.uniform(jax.random.fold_in(jax.random.fold_in(key, 6), dim), (blocks,), jnp.float32, smallest / len(cuts), largest / len(cuts))
        return jnp.repeat(jnp.exp(steps), shape[dim] // blocks).reshape((-1,) + (1,) * (len(shape) - dim - 1))

    level = one(*cuts[0])
    for cut in cuts[1:]:
        level = level * one(*cut)
    return level


def split_up(count, total, most, slope):
    weights = [(1 << 20) // math.isqrt(rank ** slope) + 1 for rank in range(2, count + 1)]
    rest, holding = total - most - (count - 1), [1] * (count - 1)
    while rest > 0:
        movable = [i for i in range(count - 1) if holding[i] < most]
        mass, remaining = sum([weights[i] for i in movable]), rest
        for i in movable:
            extra = min(most - holding[i], max(1, remaining * weights[i] // mass), rest)
            holding[i] = holding[i] + extra
            rest = rest - extra
    return np.array([most] + holding)


def uneven_parts(own_key, number_of, total, bound, slope):
    if number_of == 2:
        one = jax.random.randint(own_key, (), max(1, total - bound), min(bound, total - 1) + 1)
        return jnp.stack([one, total - one])
    sizes = jnp.asarray(split_up(number_of, total, bound, slope), jnp.int32)
    pairs = (number_of - 1) // 2
    giver, receiver = sizes[1:1 + 2 * pairs:2], sizes[2:2 + 2 * pairs:2]
    room = jnp.minimum(giver - 1, bound - receiver)
    passed = jax.random.randint(jax.random.fold_in(own_key, 1), (pairs,), 0, 1 << 20) % (room + 1)
    sizes = sizes.at[1:1 + 2 * pairs:2].set(giver - passed).at[2:2 + 2 * pairs:2].set(receiver + passed)
    return sizes[jax.random.permutation(jax.random.fold_in(own_key, 2), number_of)]


def shared_out(key, own, number, rows, count, top, reach, skew):
    order = jax.random.permutation(key, count)
    heavy_load, common = shares(count, rows * top, reach, skew, True), shares(count, rows * top, reach, skew, False)
    places = jnp.arange(count)

    def named(sizes, turn):
        used = int((sizes > 0).sum())
        fixed = max(1, used // 4)
        moved = fixed + (places - fixed + turn * (used - fixed)) % max(1, count - fixed)
        return jnp.zeros((count,), jnp.int32).at[order[jnp.where(places < fixed, places, moved)]].set(jnp.asarray(sizes, jnp.int32))

    sizes = jnp.where(number % 4 == 0, named(heavy_load, number // 4), named(common, number - number // 4 - 1))
    mixed = jax.random.permutation(jax.random.fold_in(own, 3), count)
    source_of, receiver = mixed[0:count // 2 * 2:2], mixed[1:count // 2 * 2:2]
    room = jnp.minimum(sizes[source_of] - 1, reach - sizes[receiver]) // 2
    room = jnp.where((source_of == order[0]) | (receiver == order[0]) | (sizes[receiver] == 0), 0, jnp.maximum(room, 0))
    moved = jax.random.randint(jax.random.fold_in(own, 4), (count // 2,), 0, 1 << 20) % (room + 1)
    sizes = sizes.at[source_of].add(-moved).at[receiver].add(moved)
    members = jnp.searchsorted(jnp.cumsum(sizes), jnp.arange(rows * top), side="right").astype(jnp.int32)
    grid = members.reshape(top, rows).T
    grid = grid[jax.random.permutation(jax.random.fold_in(own, 1), rows)]
    turn = jax.random.randint(jax.random.fold_in(own, 2), (rows, 1), 0, top)
    return jnp.take_along_axis(grid, (jnp.arange(top)[None, :] + turn) % top, axis=1)


def shares(number_of, total, reach, lean, full):
    weights = [(1 << 20) // math.isqrt(standing ** lean) + 1 for standing in range(1, number_of + 1)]
    largest = reach if full else min(reach, max(-(-total // number_of), total * weights[0] // sum(weights)))
    least = 1 if total - largest >= number_of - 1 else 0
    given, surplus = [largest] + [least] * (number_of - 1), total - largest - least * (number_of - 1)
    while surplus > 0:
        candidates = [i for i in range(1, number_of) if given[i] < largest] or [i for i in range(1, number_of) if given[i] < reach]
        whole, remaining = sum([weights[i] for i in candidates]), surplus
        for i in candidates:
            addition = min(reach - given[i], max(1, remaining * weights[i] // whole), surplus)
            given[i] = given[i] + addition
            surplus = surplus - addition
    return np.array(given)


def normal_values(own_key, shape, width, limit, cuts=(), held_as=jnp.bfloat16):
    level = steps_of(own_key, shape, cuts, -0.22, 0.18) if cuts else 1.0
    result = jax.random.normal(own_key, shape, jnp.float32) * width * level
    return jnp.minimum(jnp.maximum(result, -limit), limit).astype(held_as)


def noise_with(rng, dims, deviation, bound, cuts, heavy, kind=jnp.bfloat16):
    values = deviation * jax.random.normal(rng, dims, jnp.float32)
    if cuts:
        values = values * steps_of(rng, dims, cuts, -0.22, 0.18)
    return jnp.clip(with_spikes(values, jax.random.fold_in(rng, 3), *heavy), -bound, bound).astype(kind)


def setup_inputs(seed: int = 0) -> dict:
    key_list = jax.random.split(jax.random.key(seed), 16)
    tokens = noise_with(key_list[0], (TOKENS, D), 1.0, 6.0, ((0, 32),), (0, 1, 32, 2.75), jnp.float32)
    w_query = normal_values(key_list[1], (D, D), D ** -0.5, 0.1875, ((0, 32),), jnp.float32)
    w_key = normal_values(key_list[2], (D, D), D ** -0.5, 0.1875, ((0, 32),), jnp.float32)
    w_value = normal_values(key_list[3], (D, D), D ** -0.5, 0.1875, ((0, 32),), jnp.float32)
    w_output = normal_values(key_list[4], (D, D), (D // 64) ** -0.5, 1.5, ((0, 32),), jnp.float32)
    gain_one = jnp.clip(1.0 + 0.18 * jax.random.normal(key_list[5], (D,), jnp.float32), 0.1, 1.9)
    shift_one = normal_values(key_list[6], (D,), 0.3, 1.5, ((0, 32),), jnp.float32)
    gain_two = jnp.clip(1.0 + 0.18 * jax.random.normal(key_list[7], (D,), jnp.float32), 0.1, 1.9)
    shift_two = normal_values(key_list[8], (D,), 0.3, 1.5, ((0, 32),), jnp.float32)
    expert_in = normal_values(key_list[9], (D, EXPERTS, FFN), D ** -0.5, 0.1875, ((0, 32),), jnp.float32)
    expert_out = normal_values(key_list[10], (FFN, EXPERTS, D), FFN ** -0.5, 0.09375, ((0, 32),), jnp.float32)
    lengths = jax.vmap(lambda own: uneven_parts(own, SEQ_DEV, TOK_DEV, MAXLEN, 2))(jax.random.split(key_list[11], DEVICES)).reshape((DEVICES, SEQ_DEV)).astype(jnp.int32)
    expert_ids_keys = jax.random.split(jax.random.fold_in(key_list[12], 1), TOKENS // TOK_DEV)
    expert_ids_turns = jax.random.permutation(jax.random.fold_in(key_list[12], 3), TOKENS // TOK_DEV)
    expert_ids = jax.vmap(lambda own, number: shared_out(jax.random.fold_in(key_list[12], 2), own, number, TOK_DEV, EXPERTS, 1, CAP, 0))(expert_ids_keys, expert_ids_turns).reshape((TOKENS, 1))
    padding = with_ends((jax.random.randint(key_list[13], (TOKENS,), 0, 8) < 7).astype(jnp.int32), jax.random.fold_in(key_list[13], 1), 0, 1)
    cotangent = normal_values(key_list[14], (TOKENS, D), 1.0, 6.0, ((0, 32),), jnp.float32)
    return dict(tokens=tokens, w_query=w_query, w_key=w_key, w_value=w_value, w_output=w_output, gain_one=gain_one, shift_one=shift_one, gain_two=gain_two, shift_two=shift_two, expert_in=expert_in, expert_out=expert_out, lengths=lengths, expert_ids=expert_ids, padding=padding, cotangent=cotangent)


@jax.custom_vjp
def low(v):
    return lax.optimization_barrier(v.astype(jnp.bfloat16)).astype(jnp.float32)

@jax.custom_vjp
def low_back(v):
    return v

def low_keep(v):
    return (low(v), None)

def low_pass(kept, grad):
    return (grad,)

def back_keep(v):
    return (v, None)

def back_low(kept, grad):
    return (low(grad),)
low.defvjp(low_keep, low_pass)
low_back.defvjp(back_keep, back_low)
norm_eps = 1e-05
neg_large = -1e+30
highest_precision = lax.Precision.HIGHEST

def product(left, right):
    return jnp.dot(left, right, precision=highest_precision, preferred_element_type=jnp.float32)

def normalize(values, gain, shift):
    center = values - lax.optimization_barrier(jnp.mean(values, axis=1, keepdims=True))
    inverse = lax.rsqrt(lax.optimization_barrier(jnp.mean(center * center, axis=1, keepdims=True)) + norm_eps)
    return center * inverse * gain + shift

def expert_slots(chosen, experts, capacity):
    row_count = chosen.shape[0]
    row_order = jnp.arange(row_count, dtype=jnp.int32)
    tables = []
    for expert in range(experts):
        member = chosen == expert
        slot_place = (jnp.cumsum(member.astype(jnp.int32)) - 1).astype(jnp.int32)
        target = jnp.where(member, slot_place, capacity).astype(jnp.int32)
        tables.append(jnp.full((capacity,), row_count, jnp.int32).at[target].set(row_order, mode='drop'))
    return jnp.stack(tables)

def visible_pairs(seq_lengths, pad_rows, row_count):
    seq_ends = jnp.cumsum(seq_lengths).astype(jnp.int32)
    spots = jnp.arange(row_count, dtype=jnp.int32)
    segment = lax.optimization_barrier(jnp.sum((spots[:, None] >= seq_ends[None, :]).astype(jnp.int32), axis=1))
    same_seq = segment[:, None] == segment[None, :]
    causal = spots[None, :] <= spots[:, None]
    usable = (pad_rows[None, :] == 1) | (spots[None, :] == spots[:, None])
    return same_seq & causal & usable

def layer_forward(params, tokens, lengths, expert_ids, padding):
    rounded = [low(item) for item in params]
    w_query, w_key, w_value, w_output, gain_one, shift_one, gain_two, shift_two, w_in, w_out = rounded
    score_scale = 1.0 / math.sqrt(HEAD_DIM)

    def device_rows(pieces):
        rows_in, seq_lengths, chosen, pad_rows = pieces
        visible = visible_pairs(seq_lengths, pad_rows, TOK_DEV)
        normed = low(normalize(rows_in, gain_one, shift_one))
        queries = low_back(low(product(normed, w_query))).reshape(TOK_DEV, HEADS, HEAD_DIM)
        key_rows = low_back(low(product(normed, w_key))).reshape(TOK_DEV, HEADS, HEAD_DIM)
        value_rows = low_back(low(product(normed, w_value))).reshape(TOK_DEV, HEADS, HEAD_DIM)
        scores = jnp.einsum('qhd,khd->hqk', queries, key_rows, precision=highest_precision) * score_scale
        scores = jnp.where(visible[None], low_back(scores), neg_large)
        peak = lax.optimization_barrier(jnp.max(scores, axis=2, keepdims=True))
        shifted_exp = jnp.exp(scores - peak)
        attn_weights = low(shifted_exp / lax.optimization_barrier(jnp.sum(shifted_exp, axis=2, keepdims=True)))
        mixed = jnp.einsum('hqk,khd->qhd', attn_weights, value_rows, precision=highest_precision)
        mixed = low_back(low(mixed.reshape(TOK_DEV, D)))
        middle = rows_in + low_back(product(mixed, w_output))
        normed_two = low(normalize(middle, gain_two, shift_two))
        padded = jnp.concatenate([normed_two, jnp.zeros((1, D), jnp.float32)], axis=0)
        tables = expert_slots(chosen, EXPERTS, CAP)
        expert_sum = jnp.zeros((TOK_DEV, D), jnp.float32)
        for expert in range(EXPERTS):
            inputs = padded[tables[expert]]
            hidden = low_back(product(inputs, w_in[:, expert, :]))
            activated = low(jax.nn.gelu(hidden))
            expert_sum = expert_sum.at[tables[expert]].add(product(activated, w_out[:, expert, :]), mode='drop')
        return middle + low_back(expert_sum)
    stacked = lax.map(jax.checkpoint(device_rows), (tokens.reshape(DEVICES, TOK_DEV, D), lengths, expert_ids.reshape(DEVICES, TOK_DEV), padding.reshape(DEVICES, TOK_DEV)))
    return stacked.reshape(TOKENS, D)

def reference(tokens, w_query, w_key, w_value, w_output, gain_one, shift_one, gain_two, shift_two, expert_in, expert_out, lengths, expert_ids, padding, cotangent):
    params = (w_query, w_key, w_value, w_output, gain_one, shift_one, gain_two, shift_two, expert_in, expert_out)

    def forward_of(param_set, rows_in):
        return layer_forward(param_set, rows_in, lengths, expert_ids, padding)
    output, pullback = jax.vjp(forward_of, params, tokens)
    grad_params, grad_tokens = pullback(cotangent)
    return (output, grad_tokens, grad_params[0], grad_params[1], grad_params[2], grad_params[3], grad_params[4], grad_params[5], grad_params[6], grad_params[7], grad_params[8], grad_params[9])
```

```python
import functools
import math

import jax
import jax.numpy as jnp
from jax import lax
from jax.experimental import pallas as pl
from jax.experimental.pallas import tpu as pltpu
from jax.sharding import Mesh
from jax.sharding import PartitionSpec as P

HEADS = 16
HEAD_DIM = 64
CAP = 640
CHUNKS = 2
PARTS = 2
MIB = 1 << 20

norm_eps = 1e-05
neg_large = -1e30
gelu_c = math.sqrt(2.0 / math.pi)
gelu_k = 0.044715
f32 = jnp.float32
bf16 = jnp.bfloat16


def nt_dot(a, b):
    return lax.dot_general(a, b, (((1,), (1,)), ((), ())), preferred_element_type=f32)


def tn_dot(a, b):
    return lax.dot_general(a, b, (((0,), (0,)), ((), ())), preferred_element_type=f32)


def nn_dot(a, b):
    return jnp.dot(a, b, preferred_element_type=f32)


def params(mib, steps=1):
    return pltpu.CompilerParams(
        vmem_limit_bytes=mib * MIB, dimension_semantics=("arbitrary",) * steps
    )


def cost(us):
    return pl.CostEstimate(flops=int(us * 1.15e9), bytes_accessed=MIB, transcendentals=0)


def whole(shape, buffers=None):
    zeros = (0,) * len(shape)
    if buffers is None:
        return pl.BlockSpec(shape, lambda *_: zeros)
    return pl.BlockSpec(shape, lambda *_: zeros, pipeline_mode=pl.Buffered(buffers))


def run_kernel(kernel, *, in_specs, inputs, deps=(), prefetch=None, grid=(), out_specs, scratch_shapes=(), **rest):
    start = len(inputs) + (prefetch is not None)
    deps = list(deps)

    def body(*refs):
        kernel(*refs[:start], *refs[start + len(deps) :])

    in_specs = list(in_specs) + [pl.BlockSpec(memory_space=pl.ANY)] * len(deps)
    spec = pltpu.PrefetchScalarGridSpec(
        num_scalar_prefetch=int(prefetch is not None),
        grid=grid,
        in_specs=in_specs,
        out_specs=out_specs,
        scratch_shapes=list(scratch_shapes),
    )
    first_args = [] if prefetch is None else [prefetch]
    return pl.pallas_call(body, grid_spec=spec, **rest)(*first_args, *inputs, *deps)


def swap(value, axis):
    return lax.ppermute(value, axis, [(0, 1), (1, 0)])


class Links:
    def __init__(self, bits, fs):
        self.bits = bits
        self.fs = fs
        self.axes = tuple(f"b{k}" for k in range(bits)) + ("core",)

    def axis(self, step, core):
        return (step + core) % self.bits

    def flip(self, step, core):
        return 1 << (self.bits - 1 - self.axis(step, core))

    def mask(self, index, core):
        return sum(self.flip(t, core) for t in range(self.bits) if index >> t & 1)

    def swap(self, value, step):
        pairs = []
        for source in range(2 << self.bits):
            core = source & 1
            pairs.append((source, source ^ (self.flip(step, core) << 1)))
        return lax.ppermute(value, self.axes, pairs)

    def gather_line(self, shard):
        spread = jnp.broadcast_to(shard[None], (self.fs,) + shard.shape)
        return lax.all_to_all(spread, "fsdp", 0, 0)

    def gather_chips(self, block):
        pieces = [block]
        for t in range(self.bits):
            pieces = pieces + [self.swap(p, t) for p in pieces]
        return pieces

    def reduce_chips(self, keep, send):
        for t in reversed(range(self.bits)):
            got = self.swap(send, t)
            if t > 0:
                half = keep.shape[0] // 2
                send = add_low(keep[half:], got[half:])
                keep = add_low(keep[:half], got[:half])
            else:
                keep = add_low(keep[0], got[0])
        return keep

    def reduce_line_direct(self, value, zed):
        total = pick(value, zed, 0).astype(f32)
        for t in range(1, self.fs):
            pairs = [(z, (z + t) % self.fs) for z in range(self.fs)]
            part = lax.ppermute(pick(value, (zed + t) % self.fs, 0), "fsdp", pairs)
            total = total + part.astype(f32)
        return total

    def reduce_line(self, value):
        got = lax.all_to_all(value, "fsdp", 0, 0)
        return jnp.sum(got.astype(f32), axis=0)


def add_low(a, b):
    return (a.astype(f32) + b.astype(f32)).astype(bf16)


def norm_rows(values):
    center = values - jnp.mean(values, axis=1, keepdims=True)
    inverse = lax.rsqrt(jnp.mean(center * center, axis=1, keepdims=True) + norm_eps)
    return center * inverse, inverse


def norm_back(grad_rows, scaled, inverse, gain):
    inner = grad_rows * gain
    return inverse * (
        inner
        - jnp.mean(inner, axis=1, keepdims=True)
        - scaled * jnp.mean(inner * scaled, axis=1, keepdims=True)
    )


def load_rows(ids, pieces, rows, store):
    for i, piece in enumerate(pieces):
        store(pl.multiple_of(ids[len(pieces) // 2 + i] * rows, rows), piece)


def first_kernel(ids, tok, *refs, count, rows, width):
    pieces = refs[:count]
    h_ref, qkv_ref, w_ref, g_ref, norms = refs[count:]

    @pl.when(pl.program_id(0) == 0)
    def _():
        def store(at, piece):
            w_ref[pl.ds(at, rows), :] = piece[:, : 3 * width]
            norms[pl.ds(at, rows), :] = piece[:, 3 * width :].astype(f32)

        load_rows(ids, pieces, rows, store)
        g_ref[...] = jnp.transpose(norms[...])[:8]

    scaled, _ = norm_rows(tok[...])
    h = (scaled * g_ref[0:1, :] + g_ref[1:2, :]).astype(bf16)
    h_ref[...] = h
    for i in range(3):
        out = nn_dot(h, w_ref[:, i * width : (i + 1) * width]).astype(bf16)
        if i == 0:
            out = out * jnp.asarray(1.0 / math.sqrt(HEAD_DIM), bf16)
        qkv_ref[i] = out


def first(ids, tokens, pieces, deps):
    n, d = tokens.shape
    rows, cols = pieces[0].shape
    tile = 256
    return run_kernel(
        functools.partial(first_kernel, count=len(pieces), rows=rows, width=d),
        prefetch=ids,
        inputs=[tokens, *pieces],
        deps=deps,
        grid=(n // tile,),
        in_specs=[pl.BlockSpec((tile, d), lambda i, s: (i, 0))]
        + [whole((rows, cols), 1) for _ in pieces],
        out_specs=[
            pl.BlockSpec((tile, d), lambda i, s: (i, 0)),
            pl.BlockSpec((3, tile, d), lambda i, s: (0, i, 0)),
            whole((d, 3 * d)),
            whole((8, d)),
        ],
        scratch_shapes=[pltpu.VMEM((d, 128), f32)],
        out_shape=[
            jax.ShapeDtypeStruct((n, d), bf16),
            jax.ShapeDtypeStruct((3, n, d), bf16),
            jax.ShapeDtypeStruct((d, 3 * d), bf16),
            jax.ShapeDtypeStruct((8, d), f32),
        ],
        compiler_params=params(56),
        cost_estimate=cost(16),
        name="qkv",
    )


def make_bias(bias, kseg, qseg, n):
    key_at = lax.broadcasted_iota(jnp.int32, (256, n), 0)
    query_at = lax.broadcasted_iota(jnp.int32, (256, n), 1)
    for b in range(n // 256):
        rows = key_at + b * 256
        same = kseg[b * 256 : (b + 1) * 256, 0:1] == qseg[0:1, :]
        seen = (same & (rows <= query_at)) | (rows == query_at)
        bias[b * 256 : (b + 1) * 256, :] = jnp.where(seen, 0.0, neg_large)


def head_mask(block, head):
    lane = lax.broadcasted_iota(jnp.int32, block.shape, 1)
    return jnp.where((lane < HEAD_DIM) == (head == 0), block, jnp.zeros_like(block))


def attend_kernel(kseg, qseg, qkv, o_ref, lse_ref, bias, *, n):
    @pl.when(pl.program_id(0) == 0)
    def _():
        make_bias(bias, kseg, qseg, n)

    k = qkv[1]
    v_t = jnp.transpose(qkv[2])
    for i in range(n // 256):
        keys = (i + 1) * 256
        cols = slice(i * 256, keys)
        q = qkv[0, cols, :]
        parts = []
        for head in range(2):
            s = nt_dot(k[:keys], head_mask(q, head)) + bias[:keys, cols]
            peak = jnp.max(s, axis=0, keepdims=True)
            e = jnp.exp(s - peak)
            total = jnp.sum(e, axis=0, keepdims=True)
            p = (e * (1.0 / total)).astype(bf16)
            parts.append(nn_dot(v_t[head * HEAD_DIM : (head + 1) * HEAD_DIM, :keys], p))
            lse_ref[0, head : head + 1, cols] = peak + jnp.log(total)
        o_ref[cols, :] = jnp.transpose(jnp.concatenate(parts, axis=0)).astype(bf16)


def attend(kseg, qseg, qkv, part, parts, deps):
    _, n, d = qkv.shape
    pairs = d // 128 // parts
    d = d // parts
    return run_kernel(
        functools.partial(attend_kernel, n=n),
        inputs=[kseg, qseg, qkv],
        deps=deps,
        grid=(pairs,),
        in_specs=[
            whole(kseg.shape),
            whole(qseg.shape),
            pl.BlockSpec((3, n, 128), lambda p: (0, 0, p + part * pairs)),
        ],
        out_specs=[
            pl.BlockSpec((n, 128), lambda p: (0, p)),
            pl.BlockSpec((1, 8, n), lambda p: (p, 0, 0)),
        ],
        out_shape=[
            jax.ShapeDtypeStruct((n, d), bf16),
            jax.ShapeDtypeStruct((pairs, 8, n), f32),
        ],
        scratch_shapes=[pltpu.VMEM((n, n), f32)],
        compiler_params=params(48),
        cost_estimate=cost(21),
        name="attend",
    )


def attend_back_kernel(kseg, qseg, qkv, do_ref, lse_ref, out, bias, dk_acc, dv_acc, *, n):
    @pl.when(pl.program_id(0) == 0)
    def _():
        make_bias(bias, kseg, qseg, n)

    k = qkv[1]
    v = qkv[2]
    k_t = jnp.transpose(k)
    blocks = n // 256
    for i in reversed(range(blocks)):
        keys = (i + 1) * 256
        cols = slice(i * 256, keys)
        parts = []
        for head in range(2):
            q = head_mask(qkv[0, cols, :], head)
            go = head_mask(do_ref[cols, :], head)
            s = nt_dot(k[:keys], q) + bias[:keys, cols]
            p = jnp.exp(s - lse_ref[0, head : head + 1, cols])
            dp = nt_dot(v[:keys], go)
            inner = jnp.sum(p * dp, axis=0, keepdims=True)
            ds = (p * (dp - inner)).astype(bf16)
            dv = nn_dot(p.astype(bf16), go)
            dk = nn_dot(ds, q)
            if i == blocks - 1 and head == 0:
                dv_acc[...] = dv
                dk_acc[...] = dk
            else:
                dv_acc[:keys, :] += dv
                dk_acc[:keys, :] += dk
            parts.append(nn_dot(k_t[head * HEAD_DIM : (head + 1) * HEAD_DIM, :keys], ds))
        dq = jnp.concatenate(parts, axis=0) * (1.0 / math.sqrt(HEAD_DIM))
        out[0, cols, :] = jnp.transpose(dq).astype(bf16)
    out[1] = dk_acc[...].astype(bf16)
    out[2] = dv_acc[...].astype(bf16)


def attend_back(kseg, qseg, qkv, grad_mixed, lse, part, parts, deps):
    _, n, d = qkv.shape
    pairs = d // 128 // parts
    d = d // parts
    return run_kernel(
        functools.partial(attend_back_kernel, n=n),
        inputs=[kseg, qseg, qkv, grad_mixed, lse],
        deps=deps,
        grid=(pairs,),
        in_specs=[
            whole(kseg.shape),
            whole(qseg.shape),
            pl.BlockSpec((3, n, 128), lambda p: (0, 0, p + part * pairs)),
            pl.BlockSpec((n, 128), lambda p: (0, p + part * pairs)),
            pl.BlockSpec((1, 8, n), lambda p: (p, 0, 0)),
        ],
        out_specs=pl.BlockSpec((3, n, 128), lambda p: (0, 0, p)),
        out_shape=jax.ShapeDtypeStruct((3, n, d), bf16),
        scratch_shapes=[
            pltpu.VMEM((n, n), f32),
            pltpu.VMEM((n, 128), f32),
            pltpu.VMEM((n, 128), f32),
        ],
        compiler_params=params(56),
        cost_estimate=cost(11),
        name="attend_back",
    )


def slot_hot(slot_row, start, count):
    n = slot_row.shape[1]
    at = lax.broadcasted_iota(jnp.int32, (count, n), 0) + start
    return jnp.where(at == slot_row, 1.0, 0.0).astype(bf16)


def pack_kernel(slot_row, values, own, other):
    low = values[...].astype(bf16)
    own[...] = nn_dot(slot_hot(slot_row[0:1, :], 0, CAP), low).astype(bf16)
    other[...] = nn_dot(slot_hot(slot_row[0:1, :], CAP, CAP), low).astype(bf16)


def pack(slot_row, values):
    n, d = values.shape
    return pl.pallas_call(
        pack_kernel,
        in_specs=[whole(slot_row.shape), whole((n, d))],
        out_specs=[whole((CAP, d))] * 2,
        out_shape=[jax.ShapeDtypeStruct((CAP, d), bf16)] * 2,
        compiler_params=pltpu.CompilerParams(vmem_limit_bytes=48 * MIB),
        cost_estimate=cost(5),
        name="pack",
    )(slot_row, values)


def second_kernel(ids, slot_row, tok, gains, *refs, count, rows, steps, tile, parts):
    mixed, refs = refs[:parts], refs[parts:]
    pieces = refs[:count]
    x_ref, w_ref, own, other, h_all = refs[count:]
    step = pl.program_id(0)

    @pl.when(step == 0)
    def _():
        def store(at, piece):
            w_ref[pl.ds(at, rows), :] = piece[...]

        load_rows(ids, pieces, rows, store)

    x = tok[...]
    wide = mixed[0].shape[1]
    for i, o_ref in enumerate(mixed):
        x = x + nn_dot(o_ref[...], w_ref[i * wide : (i + 1) * wide, :])
    x_ref[...] = x
    scaled, _ = norm_rows(x)
    h = (scaled * gains[2:3, :] + gains[3:4, :]).astype(bf16)
    h_all[pl.ds(pl.multiple_of(step * tile, tile), tile), :] = h

    @pl.when(step == steps - 1)
    def _():
        own[...] = nn_dot(slot_hot(slot_row[0:1, :], 0, CAP), h_all[...]).astype(bf16)
        other[...] = nn_dot(slot_hot(slot_row[0:1, :], CAP, CAP), h_all[...]).astype(bf16)


def second(ids, slot_row, mixed, tokens, gains, pieces, deps):
    n, d = tokens.shape
    rows, _ = pieces[0].shape
    tile = 256
    return run_kernel(
        functools.partial(
            second_kernel, count=len(pieces), rows=rows, steps=n // tile, tile=tile, parts=len(mixed)
        ),
        prefetch=ids,
        inputs=[slot_row, tokens, gains, *mixed, *pieces],
        deps=deps,
        **dict(
            grid=(n // tile,),
            in_specs=[
                whole(slot_row.shape),
                pl.BlockSpec((tile, d), lambda i, s: (i, 0)),
                whole(gains.shape),
            ]
            + [pl.BlockSpec((tile, o.shape[1]), lambda i, s: (i, 0)) for o in mixed]
            + [whole((rows, d), 1) for _ in pieces],
            out_specs=[
                pl.BlockSpec((tile, d), lambda i, s: (i, 0)),
                whole((d, d)),
                whole((CAP, d)),
                whole((CAP, d)),
            ],
            scratch_shapes=[pltpu.VMEM((n, d), bf16)],
        ),
        out_shape=[
            jax.ShapeDtypeStruct((n, d), f32),
            jax.ShapeDtypeStruct((d, d), bf16),
            jax.ShapeDtypeStruct((CAP, d), bf16),
            jax.ShapeDtypeStruct((CAP, d), bf16),
        ],
        compiler_params=params(56),
        cost_estimate=cost(13),
        name="mix_out",
    )


def expert_kernel(ids, *refs, count, rows, tile, first_chunk, block):
    half = count // 2
    xs, ys = refs[0:2], refs[2:4]
    pos = 4
    prior = None
    if not first_chunk:
        prior = refs[pos : pos + 4]
        pos += 4
    pieces = refs[pos : pos + count]
    pos += count
    y_out, h_out = refs[pos : pos + 2], refs[pos + 2 : pos + 4]
    keep, send = refs[pos + 4 : pos + 6]
    x_s, dy_s, win_s, wout_s, y_acc, h_acc, a_s, du_s, sems = refs[pos + 6 :]
    step = pl.program_id(0)
    d = x_s.shape[1]
    slabs = win_s.shape[1] // d
    total = 2 * CAP

    @pl.when(step == 0)
    def _():
        copies = []

        def fetch(source, target):
            copy = pltpu.make_async_copy(source, target, sems.at[len(copies)])
            copy.start()
            copies.append(copy)

        for side in range(2):
            fetch(xs[side], x_s.at[pl.ds(side * CAP, CAP)])
        for i in range(count):
            at = pl.multiple_of(ids[i] * rows, rows)
            for h in range(slabs):
                fetch(
                    pieces[i].at[pl.ds(h * rows, rows)],
                    win_s.at[pl.ds(at, rows), pl.ds(h * d, d)],
                )
        for side in range(2):
            fetch(ys[side], dy_s.at[pl.ds(side * CAP, CAP)])
        for i in range(count):
            at = pl.multiple_of(ids[i] * tile, tile)
            fetch(pieces[i].at[pl.ds(slabs * rows, tile)], wout_s.at[pl.ds(at, tile)])
        if first_chunk:
            y_acc[...] = jnp.zeros_like(y_acc)
            h_acc[...] = jnp.zeros_like(h_acc)
        else:
            for side in range(2):
                span = slice(side * CAP, (side + 1) * CAP)
                y_acc[span, :] = prior[side][...].astype(f32)
                h_acc[span, :] = prior[2 + side][...].astype(f32)
        for copy in copies:
            copy.wait()

    at = pl.multiple_of(ids[step] * tile, tile)

    def one_block(b, carry):
        span = pl.ds(pl.multiple_of(b * block, block), block)
        u = nn_dot(x_s[span, :], win_s[:, pl.ds(at, tile)])
        da = nt_dot(dy_s[span, :], wout_s[pl.ds(at, tile), :])
        square = u * u
        t = jnp.tanh(gelu_c * (u * (1.0 + gelu_k * square)))
        up = 0.5 * (1.0 + t)
        slope = up + (0.5 * gelu_c) * u * (1.0 - t * t) * (1.0 + 3.0 * gelu_k * square)
        a = (u * up).astype(bf16)
        du = (da * slope).astype(bf16)
        a_s[span, :] = a
        du_s[span, :] = du
        y_acc[span, :] += nn_dot(a, wout_s[pl.ds(at, tile), :])
        h_acc[span, :] += nt_dot(du, win_s[:, pl.ds(at, tile)])
        return carry

    lax.fori_loop(0, total // block, one_block, 0)
    grad = tn_dot(a_s[...], dy_s[...]).astype(bf16)

    @pl.when(step < half)
    def _():
        keep[step, slabs * rows :, :] = grad

    @pl.when(step >= half)
    def _():
        send[step - half, slabs * rows :, :] = grad

    slab = at // d
    row = pl.multiple_of(slab * rows, rows)
    col = pl.multiple_of(at - slab * d, tile)

    def one_piece(i, carry):
        for out, index in ((keep, i), (send, i + half)):
            src = pl.multiple_of(ids[index] * rows, rows)
            out[i, pl.ds(row, rows), pl.ds(col, tile)] = tn_dot(
                x_s[:, pl.ds(src, rows)], du_s[...]
            ).astype(bf16)
        return carry

    lax.fori_loop(0, half, one_piece, 0)

    @pl.when(step == count - 1)
    def _():
        for side in range(2):
            span = slice(side * CAP, (side + 1) * CAP)
            y_out[side][...] = y_acc[span, :].astype(bf16)
            h_out[side][...] = h_acc[span, :].astype(bf16)


def expert(ids, xs, ys, prior, pieces, rows, tile, deps):
    count = len(pieces)
    half = count // 2
    d = xs[0].shape[1]
    hc = count * tile
    total = 2 * CAP
    first_chunk = prior is None
    far = pl.BlockSpec(memory_space=pl.ANY)
    both = (half,) + pieces[0].shape
    return run_kernel(
        functools.partial(
            expert_kernel, count=count, rows=rows, tile=tile, first_chunk=first_chunk, block=320
        ),
        prefetch=ids,
        inputs=list(xs) + list(ys) + list(prior or ()) + list(pieces),
        deps=deps,
        grid=(count,),
        in_specs=[far] * 4
        + ([] if first_chunk else [whole((CAP, d), 1)] * 4)
        + [far] * count,
        out_specs=[whole((CAP, d), 1)] * 4 + [whole(both, 1)] * 2,
        scratch_shapes=[
            pltpu.VMEM((total, d), bf16),
            pltpu.VMEM((total, d), bf16),
            pltpu.VMEM((d, hc), bf16),
            pltpu.VMEM((hc, d), bf16),
            pltpu.VMEM((total, d), f32),
            pltpu.VMEM((total, d), f32),
            pltpu.VMEM((total, tile), bf16),
            pltpu.VMEM((total, tile), bf16),
            pltpu.SemaphoreType.DMA((4 + (hc // d + 1) * count,)),
        ],
        out_shape=[jax.ShapeDtypeStruct((CAP, d), bf16)] * 4
        + [jax.ShapeDtypeStruct(both, bf16)] * 2,
        compiler_params=params(60),
        cost_estimate=cost(27),
        name="experts",
    )


def third_kernel(slot_col, gains, x_ref, cot, w_ref, *refs):
    y_own, y_other, h_own, h_other = refs[:4]
    out_ref, mid_ref, dz_ref, do_ref, g_ref = refs[4:]
    tile = x_ref.shape[0]
    at = lax.broadcasted_iota(jnp.int32, (tile, CAP), 1)
    own = jnp.where(slot_col[:, 0:1] == at, 1.0, 0.0).astype(bf16)
    other = jnp.where(slot_col[:, 0:1] == at + CAP, 1.0, 0.0).astype(bf16)
    x = x_ref[...]
    out_ref[...] = x + nn_dot(own, y_own[...]) + nn_dot(other, y_other[...])
    dh = nn_dot(own, h_own[...]) + nn_dot(other, h_other[...])
    scaled, inverse = norm_rows(x)
    mid = cot[...] + norm_back(dh, scaled, inverse, gains[2:3, :])
    mid_ref[...] = mid
    dz = mid.astype(bf16)
    dz_ref[...] = dz
    do_ref[...] = nt_dot(dz, w_ref[...]).astype(bf16)

    @pl.when(pl.program_id(0) == 0)
    def _():
        g_ref[...] = jnp.zeros_like(g_ref)

    g_ref[0:1, :] += jnp.sum(dh * scaled, axis=0, keepdims=True)
    g_ref[1:2, :] += jnp.sum(dh, axis=0, keepdims=True)


def third(slot_col, gains, middle, cot, w_out, returned, deps):
    n, d = middle.shape
    tile = 256
    row = pl.BlockSpec((tile, d), lambda i: (i, 0))
    return run_kernel(
        third_kernel,
        inputs=[slot_col, gains, middle, cot, w_out, *returned],
        deps=deps,
        grid=(n // tile,),
        in_specs=[
            pl.BlockSpec((tile, slot_col.shape[1]), lambda i: (i, 0)),
            whole(gains.shape),
            row,
            row,
            whole((d, d), 1),
        ]
        + [whole((CAP, d), 1)] * 4,
        out_specs=[row, row, row, row, whole((8, d))],
        out_shape=[
            jax.ShapeDtypeStruct((n, d), f32),
            jax.ShapeDtypeStruct((n, d), f32),
            jax.ShapeDtypeStruct((n, d), bf16),
            jax.ShapeDtypeStruct((n, d), bf16),
            jax.ShapeDtypeStruct((8, d), f32),
        ],
        compiler_params=params(56),
        cost_estimate=cost(8),
        name="combine",
    )


def weights_kernel(ids, right, *refs, count, rows, lefts):
    keep, send, left_t, res = refs[lefts:]

    @pl.when(pl.program_id(0) == 0)
    def _():
        wide = refs[0].shape[1]
        for i in range(lefts):
            left_t[i * wide : (i + 1) * wide, :] = jnp.transpose(refs[i][...])

    res[...] = nn_dot(left_t[...], right[0])
    for i in range(count):
        for out, r in ((keep, count + i), (send, 2 * count + i)):
            src = pl.multiple_of(ids[r] * rows, rows)
            out[i] = res[pl.ds(src, rows), :].astype(bf16)


def weights(ids, lefts, right, count, deps=(), tile=512):
    n = right.shape[1]
    d = sum(left.shape[1] for left in lefts)
    parts, _, wide = right.shape
    per = wide // tile
    rows = d // (2 * count)
    out = pl.BlockSpec((count, rows, tile), lambda j, s: (0, 0, j))
    return run_kernel(
        functools.partial(weights_kernel, count=count, rows=rows, lefts=len(lefts)),
        prefetch=ids,
        inputs=[right, *lefts],
        deps=deps,
        grid=(parts * per,),
        in_specs=[pl.BlockSpec((1, n, tile), lambda j, s: (j // per, 0, j % per))]
        + [whole(left.shape, 1) for left in lefts],
        out_specs=[out, out],
        scratch_shapes=[pltpu.VMEM((d, n), bf16), pltpu.VMEM((d, tile), f32)],
        out_shape=[jax.ShapeDtypeStruct((count, rows, parts * wide), bf16)] * 2,
        compiler_params=params(48),
        cost_estimate=cost(4),
        name="weight_grads",
    )


def last_kernel(gains, tok, mid, w_ref, *refs):
    grads, (out_ref, g_ref) = refs[:-2], refs[-2:]
    d = tok.shape[1]
    wide = grads[0].shape[2]
    dh = None
    for j, grad in enumerate(grads):
        for i in range(3):
            at = i * d + j * wide
            term = nt_dot(grad[i], w_ref[:, at : at + wide])
            dh = term if dh is None else dh + term
    scaled, inverse = norm_rows(tok[...])
    out_ref[...] = mid[...] + norm_back(dh, scaled, inverse, gains[0:1, :])

    @pl.when(pl.program_id(0) == 0)
    def _():
        g_ref[...] = jnp.zeros_like(g_ref)

    g_ref[0:1, :] += jnp.sum(dh * scaled, axis=0, keepdims=True)
    g_ref[1:2, :] += jnp.sum(dh, axis=0, keepdims=True)


def last(gains, tokens, middle_grad, dqkv, w_qkv, deps):
    n, d = tokens.shape
    tile = 256
    row = pl.BlockSpec((tile, d), lambda i: (i, 0))
    return run_kernel(
        last_kernel,
        inputs=[gains, tokens, middle_grad, w_qkv, *dqkv],
        deps=deps,
        grid=(n // tile,),
        in_specs=[
            whole(gains.shape),
            row,
            row,
            whole((d, 3 * d), 1),
        ]
        + [pl.BlockSpec((3, tile, g.shape[2]), lambda i: (0, i, 0)) for g in dqkv],
        out_specs=[row, whole((8, d))],
        out_shape=[jax.ShapeDtypeStruct((n, d), f32), jax.ShapeDtypeStruct((8, d), f32)],
        compiler_params=params(48),
        cost_estimate=cost(8),
        name="token_grads",
    )


def pick(value, index, axis):
    return lax.dynamic_index_in_dim(value, index, axis, keepdims=False)


def after(value, other):
    mark = other.reshape(-1)[0] * jnp.zeros((), other.dtype)
    return value + mark.astype(value.dtype)


def in_order(core, mine, theirs):
    return jnp.where(core == 0, jnp.stack([mine, theirs]), jnp.stack([theirs, mine]))


def local(
    tokens,
    w_query,
    w_key,
    w_value,
    w_output,
    gain_one,
    shift_one,
    gain_two,
    shift_two,
    expert_in,
    expert_out,
    lengths,
    expert_ids,
    padding,
    cotangent,
    *,
    bits,
    fs,
):
    n, d = tokens.shape
    share, _, hidden = expert_in.shape
    owned = expert_out.shape[0]
    chips = 1 << bits
    devices = 2 * chips * fs
    per = owned // CHUNKS
    hc = hidden // CHUNKS
    links = Links(bits, fs)
    core = lax.axis_index("core")
    zed = lax.axis_index("fsdp")
    chip = jnp.int32(0)
    for k in range(bits):
        chip = chip * 2 + lax.axis_index(f"b{k}")
    orders = jnp.array([[links.mask(i, c) for i in range(chips)] for c in range(2)], jnp.int32)
    near, far = chip ^ pick(orders, core, 0), chip ^ pick(orders, 1 - core, 0)
    ids = jnp.concatenate([near, near * 2 + core, far * 2 + 1 - core]).astype(jnp.int32)

    norms = jnp.stack([gain_one, shift_one, gain_two, shift_two], axis=1)
    norms = jnp.pad(norms, ((0, 0), (0, 124)))
    shard = jnp.concatenate([w_query, w_key, w_value, norms, w_output], axis=1).astype(bf16)
    line = links.gather_line(shard).reshape(fs * share, -1)

    def gather_attention(block):
        own = links.gather_chips(block)
        return own + [swap(piece, "core") for piece in own]

    qkv_pieces = gather_attention(line[:, : 3 * d + 128])
    out_pieces = gather_attention(line[:, 3 * d + 128 :])

    slabs = hc // d
    in_rows, out_rows = 2 * fs * share, 2 * fs * per
    in_low = expert_in.astype(bf16).transpose(1, 0, 2).reshape(2, share, devices, CHUNKS, per)
    in_low = in_low.transpose(0, 3, 1, 2, 4).reshape(2, CHUNKS, share, slabs, d)
    in_low = in_low.transpose(0, 1, 3, 2, 4).reshape(2, CHUNKS, slabs * share, d)
    out_low = expert_out.astype(bf16).transpose(1, 0, 2).reshape(2, CHUNKS, per, d)
    low = jnp.concatenate([in_low, out_low], axis=2)
    pair = in_order(core, pick(low, core, 0), swap(pick(low, 1 - core, 0), "core"))
    chunks, lines = [], []
    before = line
    for j in range(CHUNKS):
        got = links.gather_line(after(pair[:, j], before))
        in_part = got[:, :, : slabs * share].reshape(fs, 2, slabs, share, d)
        in_part = in_part.transpose(2, 1, 0, 3, 4).reshape(slabs * in_rows, d)
        out_part = got[:, :, slabs * share :].transpose(1, 0, 2, 3).reshape(out_rows, d)
        lines.append(jnp.concatenate([in_part, out_part], axis=0))
        chunks.append(links.gather_chips(lines[-1]))
        before = chunks[-1][1]

    spots = jnp.arange(n, dtype=jnp.int32)
    eight = jnp.arange(lengths.shape[1])
    ends = jnp.sum(jnp.where(eight[:, None] <= eight[None, :], lengths[0][:, None], 0), axis=0)
    segment = jnp.sum((spots[:, None] >= ends[None, :]).astype(jnp.int32), axis=1)
    key_segment = jnp.where(padding == 1, segment, -1)
    kseg = jnp.broadcast_to(key_segment[:, None], (n, 128))
    qseg = jnp.broadcast_to(segment[None, :], (8, n))
    chosen = expert_ids[:, 0]
    names = jnp.arange(2, dtype=jnp.int32)
    hot = (chosen[:, None] == names[None, :]).astype(bf16)
    before = (spots[:, None] > spots[None, :]).astype(bf16)
    place = nn_dot(before, hot).astype(jnp.int32)
    place = jnp.where(chosen == 0, place[:, 0], place[:, 1])
    slot = jnp.where(chosen == core, place, CAP + place)
    slot_row = jnp.broadcast_to(slot[None, :], (8, n))
    slot_col = jnp.broadcast_to(slot[:, None], (n, 128))

    dy_own, dy_other = pack(slot_row, cotangent)
    dys = (dy_own, swap(dy_other, "core"))
    h1, qkv, w_qkv, gains = first(ids, tokens, qkv_pieces, [lines[0]])
    mixed, lse = [], []
    needs = [[chunks[0][1], *out_pieces[chips:]], []]
    for i in range(PARTS):
        made = attend(kseg, qseg, qkv, i, PARTS, needs[i] + lse[-1:])
        mixed.append(made[0])
        lse.append(made[1])
    middle, w_out, x_own, x_other = second(ids, slot_row, mixed, tokens, gains, out_pieces, [lines[1]])
    xs = (x_own, swap(x_other, "core"))

    def chip_rows(keep, send):
        t = bits - 1
        got = links.swap(send, t)
        while t > 0:
            half = keep.shape[0] // 2
            send, keep = add_low(keep[half:], got[half:]), add_low(keep[:half], got[:half])
            yield send
            t -= 1
            got = links.swap(send, t)
        total = add_low(keep[0], got[0])
        in_part = total[: slabs * in_rows].reshape(slabs, 2, fs, share, d)
        in_part = in_part.transpose(2, 1, 0, 3, 4).reshape(fs, 2, slabs * share, d)
        out_part = total[slabs * in_rows :].reshape(2, fs, per, d).transpose(1, 0, 2, 3)
        total = jnp.concatenate([in_part, out_part], axis=2)
        yield total
        yield links.reduce_line(total)

    made = expert(ids, xs, dys, None, chunks[0], in_rows, out_rows, [chunks[1][1]])
    stages = [list(chip_rows(made[4], made[5]))]
    made = expert(ids, xs, dys, made[:4], chunks[1], in_rows, out_rows, [])
    stages.append(list(chip_rows(made[4], made[5])))
    y_own, y_far, h_own, h_far = made[:4]
    returned = (y_own, swap(y_far, "core"), h_own, swap(h_far, "core"))

    output, grad_middle, dz, grad_mixed, sums_two = third(
        slot_col, gains, middle, cotangent, w_out, returned, [stages[0][0]]
    )

    def attention_rows(keep, send):
        keep = add_low(keep, swap(send, "core"))
        half = chips // 2
        yield keep
        got = links.reduce_chips(keep[:half], keep[half:])
        yield got.reshape(fs, share, -1)

    wide = d // PARTS
    made = weights(ids, mixed, dz[None], chips)
    out_stages = list(attention_rows(*made))
    grads, qkv_stages = [], []
    needs = [[stages[0][-2]], [stages[1][0]]]
    for i in range(PARTS):
        grads.append(
            attend_back(kseg, qseg, qkv, grad_mixed, lse[i], i, PARTS, needs[i] + [made[1]])
        )
        made = weights(ids, [h1], grads[i], chips, [[out_stages[0]], [stages[0][-1], stages[1][-2]]][i])
        qkv_stages.append(list(attention_rows(*made)))
    grad_tokens, sums_one = last(
        gains, tokens, grad_middle, grads, w_qkv, [made[1], qkv_stages[0][-1], out_stages[-1]]
    )
    ready = [g[-1] for g in qkv_stages] + [out_stages[-1]]
    ready = links.reduce_line_direct(jnp.concatenate(ready, axis=2), zed)
    grad_qkv = [
        jnp.concatenate(
            [ready[:, (3 * j + i) * wide : (3 * j + i + 1) * wide] for j in range(PARTS)], axis=1
        )
        for i in range(3)
    ]
    grad_output = ready[:, 3 * d :]

    def settle(rows):
        return in_order(core, pick(rows, core, 0), swap(pick(rows, 1 - core, 0), "core"))

    totals = [settle(s[-1]) for s in stages]
    grad_expert_in = jnp.stack(
        [g[:, : slabs * share].reshape(2, slabs, share, d) for g in totals], axis=0
    )
    grad_expert_in = grad_expert_in.transpose(3, 1, 0, 2, 4).reshape(share, 2, CHUNKS, devices, per)
    grad_expert_in = grad_expert_in.transpose(0, 1, 3, 2, 4).reshape(share, 2, hidden)
    grad_expert_out = jnp.stack([g[:, slabs * share :] for g in totals], axis=1)
    grad_expert_out = grad_expert_out.reshape(2, owned, d).transpose(1, 0, 2)

    sums = jnp.concatenate([sums_one[:2], sums_two[:2]]).reshape(4, devices, share).transpose(1, 0, 2)
    sums = jnp.sum(lax.all_to_all(sums, links.axes + ("fsdp",), 0, 0), axis=0)

    return (
        output,
        grad_tokens,
        grad_qkv[0],
        grad_qkv[1],
        grad_qkv[2],
        grad_output,
        sums[0],
        sums[1],
        sums[2],
        sums[3],
        grad_expert_in,
        grad_expert_out,
    )


def solution(mesh):
    dp, fs = mesh.shape["dp"], mesh.shape["fsdp"]
    bits = (dp // 2).bit_length() - 1
    names = tuple(f"b{k}" for k in range(bits)) + ("core", "fsdp")
    fine = Mesh(mesh.devices.reshape((2,) * (bits + 1) + (fs,)), names)
    rows = lambda rank: P(names, *([None] * (rank - 1)))
    in_specs = tuple(rows(r) for r in (2, 2, 2, 2, 2, 1, 1, 1, 1, 3, 3, 2, 2, 1, 2))
    out_specs = tuple(rows(r) for r in (2, 2, 2, 2, 2, 2, 1, 1, 1, 1, 3, 3))
    return jax.shard_map(
        functools.partial(local, bits=bits, fs=fs),
        mesh=fine,
        in_specs=in_specs,
        out_specs=out_specs,
        check_vma=False,
    )
```

```python
import functools
import math

import jax
import jax.numpy as jnp
from jax import lax
from jax.experimental import pallas as pl
from jax.experimental.pallas import tpu as pltpu
from jax.sharding import Mesh
from jax.sharding import PartitionSpec as P

HEADS = 16
HEAD_DIM = 64
CAP = 640
PARTS = 2
MIB = 1 << 20

norm_eps = 1e-05
neg_large = -1e30
gelu_c = math.sqrt(2.0 / math.pi)
gelu_k = 0.044715
f32 = jnp.float32
bf16 = jnp.bfloat16


def nt_dot(a, b):
    return lax.dot_general(a, b, (((1,), (1,)), ((), ())), preferred_element_type=f32)


def tn_dot(a, b):
    return lax.dot_general(a, b, (((0,), (0,)), ((), ())), preferred_element_type=f32)


def nn_dot(a, b):
    return jnp.dot(a, b, preferred_element_type=f32)


def params(mib, steps=1):
    return pltpu.CompilerParams(
        vmem_limit_bytes=mib * MIB, dimension_semantics=("arbitrary",) * steps
    )


def cost(us):
    return pl.CostEstimate(flops=int(us * 1.15e9), bytes_accessed=MIB, transcendentals=0)


def whole(shape, buffers=None):
    zeros = (0,) * len(shape)
    if buffers is None:
        return pl.BlockSpec(shape, lambda *_: zeros)
    return pl.BlockSpec(shape, lambda *_: zeros, pipeline_mode=pl.Buffered(buffers))


def run_kernel(
    kernel, *, in_specs, inputs, out_specs, out_shape, deps=(), through=(), prefetch=None, grid=(), scratch_shapes=(), **rest
):
    first_args = [] if prefetch is None else [prefetch]
    deps, through = list(deps), list(through)
    out_specs = list(out_specs) if isinstance(out_specs, (list, tuple)) else [out_specs]
    out_shape = list(out_shape) if isinstance(out_shape, (list, tuple)) else [out_shape]
    a = len(first_args) + len(inputs)
    b = a + len(deps) + len(through)
    c = b + len(out_shape)

    def body(*refs):
        kernel(*refs[:a], *refs[b:c], *refs[c + len(through) :])

    far = pl.BlockSpec(memory_space=pl.ANY)
    spec = pltpu.PrefetchScalarGridSpec(
        num_scalar_prefetch=len(first_args),
        grid=grid,
        in_specs=list(in_specs) + [far] * (b - a),
        out_specs=out_specs + [far] * len(through),
        scratch_shapes=list(scratch_shapes),
    )
    made = pl.pallas_call(
        body,
        grid_spec=spec,
        out_shape=out_shape + [jax.ShapeDtypeStruct(t.shape, t.dtype) for t in through],
        input_output_aliases={a + len(deps) + i: len(out_shape) + i for i in range(len(through))},
        **rest,
    )(*first_args, *inputs, *deps, *through)
    return made if len(made) > 1 else made[0]


def swap(value, axis):
    return lax.ppermute(value, axis, [(0, 1), (1, 0)])


class Links:
    def __init__(self, bits, fs):
        self.bits = bits
        self.fs = fs
        self.axes = tuple(f"b{k}" for k in range(bits)) + ("core",)

    def axis(self, step, core):
        return (step + core) % self.bits

    def flip(self, step, core):
        return 1 << (self.bits - 1 - self.axis(step, core))

    def mask(self, index, core):
        return sum(self.flip(t, core) for t in range(self.bits) if index >> t & 1)

    def swap(self, value, step):
        pairs = []
        for source in range(2 << self.bits):
            core = source & 1
            pairs.append((source, source ^ (self.flip(step, core) << 1)))
        return lax.ppermute(value, self.axes, pairs)

    def gather_line(self, shard):
        spread = jnp.broadcast_to(shard[None], (self.fs,) + shard.shape)
        return lax.all_to_all(spread, "fsdp", 0, 0)

    def gather_chips(self, block):
        pieces = [block]
        for t in range(self.bits):
            pieces = pieces + [self.swap(p, t) for p in pieces]
        return pieces

    def reduce_chips(self, keep, send, steps):
        for t in reversed(range(steps)):
            got = self.swap(send, t)
            if t > 0:
                half = keep.shape[0] // 2
                send = add_low(keep[half:], got[half:])
                keep = add_low(keep[:half], got[:half])
            else:
                keep = add_low(keep[0], got[0])
        return keep

    def reduce_line_direct(self, value, zed):
        total = pick(value, zed, 0).astype(f32)
        for t in range(1, self.fs):
            pairs = [(z, (z + t) % self.fs) for z in range(self.fs)]
            part = lax.ppermute(pick(value, (zed + t) % self.fs, 0), "fsdp", pairs)
            total = total + part.astype(f32)
        return total

    def reduce_line(self, value):
        got = lax.all_to_all(value, "fsdp", 0, 0)
        return jnp.sum(got.astype(f32), axis=0)


def add_low(a, b):
    return (a.astype(f32) + b.astype(f32)).astype(bf16)


def norm_rows(values):
    center = values - jnp.mean(values, axis=1, keepdims=True)
    inverse = lax.rsqrt(jnp.mean(center * center, axis=1, keepdims=True) + norm_eps)
    return center * inverse, inverse


def norm_back(grad_rows, scaled, inverse, gain):
    inner = grad_rows * gain
    return inverse * (
        inner
        - jnp.mean(inner, axis=1, keepdims=True)
        - scaled * jnp.mean(inner * scaled, axis=1, keepdims=True)
    )


def load_rows(ids, pieces, rows, store):
    for i, piece in enumerate(pieces):
        store(pl.multiple_of(ids[len(pieces) // 2 + i] * rows, rows), piece)


def first_kernel(ids, tok, *refs, count, rows, width):
    pieces = refs[:count]
    h_ref, qkv_ref, w_ref, g_ref, norms = refs[count:]

    @pl.when(pl.program_id(0) == 0)
    def _():
        def store(at, piece):
            w_ref[pl.ds(at, rows), :] = piece[:, width : 4 * width]
            norms[pl.ds(at, rows), :] = piece[:, 4 * width :].astype(f32)

        load_rows(ids, pieces, rows, store)
        g_ref[...] = jnp.transpose(norms[...])[:8]

    scaled, _ = norm_rows(tok[...])
    h = (scaled * g_ref[0:1, :] + g_ref[1:2, :]).astype(bf16)
    h_ref[...] = h
    for i in range(3):
        out = nn_dot(h, w_ref[:, i * width : (i + 1) * width]).astype(bf16)
        if i == 0:
            out = out * jnp.asarray(1.0 / math.sqrt(HEAD_DIM), bf16)
        qkv_ref[i] = out


def first(ids, tokens, pieces, deps):
    n, d = tokens.shape
    rows, cols = pieces[0].shape
    tile = 256
    return run_kernel(
        functools.partial(first_kernel, count=len(pieces), rows=rows, width=d),
        prefetch=ids,
        inputs=[tokens, *pieces],
        deps=deps,
        grid=(n // tile,),
        in_specs=[pl.BlockSpec((tile, d), lambda i, s: (i, 0))]
        + [whole((rows, cols), 1) for _ in pieces],
        out_specs=[
            pl.BlockSpec((tile, d), lambda i, s: (i, 0)),
            pl.BlockSpec((3, tile, d), lambda i, s: (0, i, 0)),
            whole((d, 3 * d)),
            whole((8, d)),
        ],
        scratch_shapes=[pltpu.VMEM((d, 128), f32)],
        out_shape=[
            jax.ShapeDtypeStruct((n, d), bf16),
            jax.ShapeDtypeStruct((3, n, d), bf16),
            jax.ShapeDtypeStruct((d, 3 * d), bf16),
            jax.ShapeDtypeStruct((8, d), f32),
        ],
        compiler_params=params(56),
        cost_estimate=cost(16),
        name="qkv",
    )


def make_bias(bias, kseg, qseg, n):
    key_at = lax.broadcasted_iota(jnp.int32, (256, n), 0)
    query_at = lax.broadcasted_iota(jnp.int32, (256, n), 1)
    for b in range(n // 256):
        rows = key_at + b * 256
        same = kseg[b * 256 : (b + 1) * 256, 0:1] == qseg[0:1, :]
        seen = (same & (rows <= query_at)) | (rows == query_at)
        bias[b * 256 : (b + 1) * 256, :] = jnp.where(seen, 0.0, neg_large)


def head_mask(block, head):
    lane = lax.broadcasted_iota(jnp.int32, block.shape, 1)
    return jnp.where((lane < HEAD_DIM) == (head == 0), block, jnp.zeros_like(block))


def attend_kernel(kseg, qseg, qkv, o_ref, lse_ref, bias, *, n):
    @pl.when(pl.program_id(0) == 0)
    def _():
        make_bias(bias, kseg, qseg, n)

    k = qkv[1]
    v_t = jnp.transpose(qkv[2])
    for i in range(n // 256):
        keys = (i + 1) * 256
        cols = slice(i * 256, keys)
        q = qkv[0, cols, :]
        parts = []
        for head in range(2):
            s = nt_dot(k[:keys], head_mask(q, head)) + bias[:keys, cols]
            peak = jnp.max(s, axis=0, keepdims=True)
            e = jnp.exp(s - peak)
            total = jnp.sum(e, axis=0, keepdims=True)
            p = (e * (1.0 / total)).astype(bf16)
            parts.append(nn_dot(v_t[head * HEAD_DIM : (head + 1) * HEAD_DIM, :keys], p))
            lse_ref[0, head : head + 1, cols] = peak + jnp.log(total)
        o_ref[cols, :] = jnp.transpose(jnp.concatenate(parts, axis=0)).astype(bf16)


def attend(kseg, qseg, qkv, part, parts, deps):
    _, n, d = qkv.shape
    pairs = d // 128 // parts
    d = d // parts
    return run_kernel(
        functools.partial(attend_kernel, n=n),
        inputs=[kseg, qseg, qkv],
        deps=deps,
        grid=(pairs,),
        in_specs=[
            whole(kseg.shape),
            whole(qseg.shape),
            pl.BlockSpec((3, n, 128), lambda p: (0, 0, p + part * pairs)),
        ],
        out_specs=[
            pl.BlockSpec((n, 128), lambda p: (0, p)),
            pl.BlockSpec((1, 8, n), lambda p: (p, 0, 0)),
        ],
        out_shape=[
            jax.ShapeDtypeStruct((n, d), bf16),
            jax.ShapeDtypeStruct((pairs, 8, n), f32),
        ],
        scratch_shapes=[pltpu.VMEM((n, n), f32)],
        compiler_params=params(48),
        cost_estimate=cost(21),
        name="attend",
    )


def attend_back_kernel(kseg, qseg, qkv, do_ref, lse_ref, out, bias, dk_acc, dv_acc, *, n):
    @pl.when(pl.program_id(0) == 0)
    def _():
        make_bias(bias, kseg, qseg, n)

    k = qkv[1]
    v = qkv[2]
    k_t = jnp.transpose(k)
    blocks = n // 256
    for i in reversed(range(blocks)):
        keys = (i + 1) * 256
        cols = slice(i * 256, keys)
        parts = []
        for head in range(2):
            q = head_mask(qkv[0, cols, :], head)
            go = head_mask(do_ref[cols, :], head)
            s = nt_dot(k[:keys], q) + bias[:keys, cols]
            p = jnp.exp(s - lse_ref[0, head : head + 1, cols])
            dp = nt_dot(v[:keys], go)
            inner = jnp.sum(p * dp, axis=0, keepdims=True)
            ds = (p * (dp - inner)).astype(bf16)
            dv = nn_dot(p.astype(bf16), go)
            dk = nn_dot(ds, q)
            if i == blocks - 1 and head == 0:
                dv_acc[...] = dv
                dk_acc[...] = dk
            else:
                dv_acc[:keys, :] += dv
                dk_acc[:keys, :] += dk
            parts.append(nn_dot(k_t[head * HEAD_DIM : (head + 1) * HEAD_DIM, :keys], ds))
        dq = jnp.concatenate(parts, axis=0) * (1.0 / math.sqrt(HEAD_DIM))
        out[0, cols, :] = jnp.transpose(dq).astype(bf16)
    out[1] = dk_acc[...].astype(bf16)
    out[2] = dv_acc[...].astype(bf16)


def attend_back(kseg, qseg, qkv, grad_mixed, lse, part, parts, deps):
    _, n, d = qkv.shape
    pairs = d // 128 // parts
    d = d // parts
    return run_kernel(
        functools.partial(attend_back_kernel, n=n),
        inputs=[kseg, qseg, qkv, grad_mixed, lse],
        deps=deps,
        grid=(pairs,),
        in_specs=[
            whole(kseg.shape),
            whole(qseg.shape),
            pl.BlockSpec((3, n, 128), lambda p: (0, 0, p + part * pairs)),
            pl.BlockSpec((n, 128), lambda p: (0, p + part * pairs)),
            pl.BlockSpec((1, 8, n), lambda p: (p, 0, 0)),
        ],
        out_specs=pl.BlockSpec((3, n, 128), lambda p: (0, 0, p)),
        out_shape=jax.ShapeDtypeStruct((3, n, d), bf16),
        scratch_shapes=[
            pltpu.VMEM((n, n), f32),
            pltpu.VMEM((n, 128), f32),
            pltpu.VMEM((n, 128), f32),
        ],
        compiler_params=params(56),
        cost_estimate=cost(22),
        name="attend_back",
    )


def slot_hot(slot_row, start, count):
    n = slot_row.shape[1]
    at = lax.broadcasted_iota(jnp.int32, (count, n), 0) + start
    return jnp.where(at == slot_row, 1.0, 0.0).astype(bf16)


def pack_kernel(slot_row, values, own, other):
    low = values[...].astype(bf16)
    own[...] = nn_dot(slot_hot(slot_row[0:1, :], 0, CAP), low).astype(bf16)
    other[...] = nn_dot(slot_hot(slot_row[0:1, :], CAP, CAP), low).astype(bf16)


def pack(slot_row, values):
    n, d = values.shape
    return pl.pallas_call(
        pack_kernel,
        in_specs=[whole(slot_row.shape), whole((n, d))],
        out_specs=[whole((CAP, d))] * 2,
        out_shape=[jax.ShapeDtypeStruct((CAP, d), bf16)] * 2,
        compiler_params=pltpu.CompilerParams(vmem_limit_bytes=48 * MIB),
        cost_estimate=cost(0.1),
        name="pack",
    )(slot_row, values)


def second_kernel(ids, slot_row, tok, gains, *refs, count, rows, steps, tile, parts):
    mixed, refs = refs[:parts], refs[parts:]
    pieces = refs[:count]
    x_ref, w_ref, own, other, h_all = refs[count:]
    step = pl.program_id(0)

    @pl.when(step == 0)
    def _():
        def store(at, piece):
            w_ref[pl.ds(at, rows), :] = piece[...]

        load_rows(ids, pieces, rows, store)

    x = tok[...]
    wide = mixed[0].shape[1]
    for i, o_ref in enumerate(mixed):
        x = x + nn_dot(o_ref[...], w_ref[i * wide : (i + 1) * wide, :])
    x_ref[...] = x
    scaled, _ = norm_rows(x)
    h = (scaled * gains[2:3, :] + gains[3:4, :]).astype(bf16)
    h_all[pl.ds(pl.multiple_of(step * tile, tile), tile), :] = h

    @pl.when(step == steps - 1)
    def _():
        own[...] = nn_dot(slot_hot(slot_row[0:1, :], 0, CAP), h_all[...]).astype(bf16)
        other[...] = nn_dot(slot_hot(slot_row[0:1, :], CAP, CAP), h_all[...]).astype(bf16)


def second(ids, slot_row, mixed, tokens, gains, pieces, deps):
    n, d = tokens.shape
    rows = pieces[0].shape[0]
    tile = 256
    return run_kernel(
        functools.partial(
            second_kernel, count=len(pieces), rows=rows, steps=n // tile, tile=tile, parts=len(mixed)
        ),
        prefetch=ids,
        inputs=[slot_row, tokens, gains, *mixed, *pieces],
        deps=deps,
        **dict(
            grid=(n // tile,),
            in_specs=[
                whole(slot_row.shape),
                pl.BlockSpec((tile, d), lambda i, s: (i, 0)),
                whole(gains.shape),
            ]
            + [pl.BlockSpec((tile, o.shape[1]), lambda i, s: (i, 0)) for o in mixed]
            + [whole((rows, d), 1) for _ in pieces],
            out_specs=[
                pl.BlockSpec((tile, d), lambda i, s: (i, 0)),
                whole((d, d)),
                whole((CAP, d)),
                whole((CAP, d)),
            ],
            scratch_shapes=[pltpu.VMEM((n, d), bf16)],
        ),
        out_shape=[
            jax.ShapeDtypeStruct((n, d), f32),
            jax.ShapeDtypeStruct((d, d), bf16),
            jax.ShapeDtypeStruct((CAP, d), bf16),
            jax.ShapeDtypeStruct((CAP, d), bf16),
        ],
        compiler_params=params(56),
        cost_estimate=cost(1),
        name="mix_out",
    )


def expert_kernel(ids, *refs, count, rows, tile, first_chunk, block):
    xs, ys = refs[0:2], refs[2:4]
    pos = 4
    prior = None
    if not first_chunk:
        prior = refs[pos : pos + 2]
        pos += 2
    pieces = refs[pos : pos + count]
    pos += count
    near, far, keep, send = refs[pos : pos + 4]
    x_s, dy_s, win_s, wout_s, y_acc, h_acc, a_s, du_s, sems = refs[pos + 4 :]
    half = count // 2
    step = pl.program_id(0)
    d = x_s.shape[1]
    slabs = win_s.shape[1] // d
    total = 2 * CAP

    @pl.when(step == 0)
    def _():
        copies = []

        def fetch(source, target):
            copy = pltpu.make_async_copy(source, target, sems.at[len(copies)])
            copy.start()
            copies.append(copy)

        for side in range(2):
            fetch(xs[side], x_s.at[pl.ds(side * CAP, CAP)])
        for i in range(count):
            at = pl.multiple_of(ids[i] * rows, rows)
            for h in range(slabs):
                fetch(
                    pieces[i].at[pl.ds(h * rows, rows)],
                    win_s.at[pl.ds(at, rows), pl.ds(h * d, d)],
                )
        for side in range(2):
            fetch(ys[side], dy_s.at[pl.ds(side * CAP, CAP)])
        for i in range(count):
            at = pl.multiple_of(ids[i] * tile, tile)
            fetch(pieces[i].at[pl.ds(slabs * rows, tile)], wout_s.at[pl.ds(at, tile)])
        if first_chunk:
            y_acc[...] = jnp.zeros_like(y_acc)
            h_acc[...] = jnp.zeros_like(h_acc)
        else:
            for side in range(2):
                span = slice(side * CAP, (side + 1) * CAP)
                y_acc[span, :] = prior[side][0].astype(f32)
                h_acc[span, :] = prior[side][1].astype(f32)
        for copy in copies:
            copy.wait()

    at = pl.multiple_of(ids[step] * tile, tile)

    def one_block(b, carry):
        span = pl.ds(pl.multiple_of(b * block, block), block)
        u = nn_dot(x_s[span, :], win_s[:, pl.ds(at, tile)])
        da = nt_dot(dy_s[span, :], wout_s[pl.ds(at, tile), :])
        square = u * u
        t = jnp.tanh(gelu_c * (u * (1.0 + gelu_k * square)))
        up = 0.5 * (1.0 + t)
        slope = up + (0.5 * gelu_c) * u * (1.0 - t * t) * (1.0 + 3.0 * gelu_k * square)
        a = (u * up).astype(bf16)
        du = (da * slope).astype(bf16)
        a_s[span, :] = a
        du_s[span, :] = du
        y_acc[span, :] += nn_dot(a, wout_s[pl.ds(at, tile), :])
        h_acc[span, :] += nt_dot(du, win_s[:, pl.ds(at, tile)])
        return carry

    lax.fori_loop(0, total // block, one_block, 0)
    grad = tn_dot(a_s[...], dy_s[...]).astype(bf16)

    for i in range(count):

        @pl.when(step == i)
        def _():
            (keep if i < half else send)[i % half, slabs * rows :, :] = grad

    slab = at // d
    row = pl.multiple_of(slab * rows, rows)
    col = pl.multiple_of(at - slab * d, tile)

    for i in range(count):
        src = pl.multiple_of(ids[i] * rows, rows)
        (keep if i < half else send)[i % half, pl.ds(row, rows), pl.ds(col, tile)] = tn_dot(
            x_s[:, pl.ds(src, rows)], du_s[...]
        ).astype(bf16)

    @pl.when(step == count - 1)
    def _():
        for side in range(2):
            span = slice(side * CAP, (side + 1) * CAP)
            (near, far)[side][0] = y_acc[span, :].astype(bf16)
            (near, far)[side][1] = h_acc[span, :].astype(bf16)


def expert(ids, xs, ys, prior, pieces, rows, tile, deps):
    count = len(pieces)
    d = xs[0].shape[1]
    hc = count * tile
    total = 2 * CAP
    first_chunk = prior is None
    far = pl.BlockSpec(memory_space=pl.ANY)
    part = (count // 2,) + pieces[0].shape
    return run_kernel(
        functools.partial(
            expert_kernel, count=count, rows=rows, tile=tile, first_chunk=first_chunk, block=320
        ),
        prefetch=ids,
        inputs=list(xs) + list(ys) + list(prior or ()) + list(pieces),
        deps=deps,
        grid=(count,),
        in_specs=[far] * 4
        + ([] if first_chunk else [whole((2, CAP, d), 1)] * 2)
        + [far] * count,
        out_specs=[whole((2, CAP, d), 1)] * 2 + [whole(part, 1)] * 2,
        scratch_shapes=[
            pltpu.VMEM((total, d), bf16),
            pltpu.VMEM((total, d), bf16),
            pltpu.VMEM((d, hc), bf16),
            pltpu.VMEM((hc, d), bf16),
            pltpu.VMEM((total, d), f32),
            pltpu.VMEM((total, d), f32),
            pltpu.VMEM((total, tile), bf16),
            pltpu.VMEM((total, tile), bf16),
            pltpu.SemaphoreType.DMA((4 + (hc // d + 1) * count,)),
        ],
        out_shape=[jax.ShapeDtypeStruct((2, CAP, d), bf16)] * 2
        + [jax.ShapeDtypeStruct(part, bf16)] * 2,
        compiler_params=params(60),
        cost_estimate=cost(53),
        name="experts",
    )


def third_kernel(slot_col, gains, x_ref, cot, w_ref, *refs):
    near, far, out_ref, mid_ref, dz_ref, do_ref, g_ref = refs
    tile = x_ref.shape[0]
    at = lax.broadcasted_iota(jnp.int32, (tile, CAP), 1)
    own = jnp.where(slot_col[:, 0:1] == at, 1.0, 0.0).astype(bf16)
    other = jnp.where(slot_col[:, 0:1] == at + CAP, 1.0, 0.0).astype(bf16)
    x = x_ref[...]
    out_ref[...] = x + nn_dot(own, near[0]) + nn_dot(other, far[0])
    dh = nn_dot(own, near[1]) + nn_dot(other, far[1])
    scaled, inverse = norm_rows(x)
    mid = cot[...] + norm_back(dh, scaled, inverse, gains[2:3, :])
    mid_ref[...] = mid
    dz = mid.astype(bf16)
    dz_ref[...] = dz
    do_ref[...] = nt_dot(dz, w_ref[...]).astype(bf16)

    @pl.when(pl.program_id(0) == 0)
    def _():
        g_ref[...] = jnp.zeros_like(g_ref)

    g_ref[0:1, :] += jnp.sum(dh * scaled, axis=0, keepdims=True)
    g_ref[1:2, :] += jnp.sum(dh, axis=0, keepdims=True)


def third(slot_col, gains, middle, cot, w_out, returned, deps, through):
    n, d = middle.shape
    tile = 256
    row = pl.BlockSpec((tile, d), lambda i: (i, 0))
    return run_kernel(
        third_kernel,
        inputs=[slot_col, gains, middle, cot, w_out, *returned],
        deps=deps,
        through=through,
        grid=(n // tile,),
        in_specs=[
            pl.BlockSpec((tile, slot_col.shape[1]), lambda i: (i, 0)),
            whole(gains.shape),
            row,
            row,
            whole((d, d), 1),
        ]
        + [whole((2, CAP, d), 1)] * 2,
        out_specs=[row, row, row, row, whole((8, d))],
        out_shape=[
            jax.ShapeDtypeStruct((n, d), f32),
            jax.ShapeDtypeStruct((n, d), f32),
            jax.ShapeDtypeStruct((n, d), bf16),
            jax.ShapeDtypeStruct((n, d), bf16),
            jax.ShapeDtypeStruct((8, d), f32),
        ],
        compiler_params=params(56),
        cost_estimate=cost(17),
        name="combine",
    )


def weights_kernel(ids, *refs, count, rows, groups, steps):
    total = sum(groups)
    lefts, rights = refs[:total], refs[total : total + len(groups)]
    keep, send, res, *turned = refs[total + len(groups) :]
    step = pl.program_id(0)

    @pl.when(step == 0)
    def _():
        k = 0
        for size, left_t in zip(groups, turned):
            wide = lefts[k].shape[1]
            for i in range(size):
                left_t[i * wide : (i + 1) * wide, :] = jnp.transpose(lefts[k + i][...])
            k += size

    start = 0
    for right, left_t, size in zip(rights, turned, steps):

        @pl.when((step >= start) & (step < start + size))
        def _():
            res[...] = nn_dot(left_t[...], right[0])

        start += size
    for i in range(count):
        for out, r in ((keep, count + i), (send, 2 * count + i)):
            src = pl.multiple_of(ids[r] * rows, rows)
            out[i] = res[pl.ds(src, rows), :].astype(bf16)


def weights(ids, products, count, us, deps=(), tile=512):
    n = products[0][1].shape[1]
    d = sum(left.shape[1] for left in products[0][0])
    rows = d // (2 * count)
    steps = [right.shape[0] * right.shape[2] // tile for _, right in products]
    in_specs = [whole(left.shape, 1) for lefts, _ in products for left in lefts]
    start = 0
    for (_, right), size in zip(products, steps):
        per = right.shape[2] // tile

        def place(j, s, start=start, size=size, per=per):
            at = jnp.clip(j - start, 0, size - 1)
            return at // per, 0, at % per

        in_specs.append(pl.BlockSpec((1, n, tile), place))
        start += size
    out = pl.BlockSpec((count, rows, tile), lambda j, s: (0, 0, j))
    return run_kernel(
        functools.partial(
            weights_kernel,
            count=count,
            rows=rows,
            groups=[len(lefts) for lefts, _ in products],
            steps=steps,
        ),
        prefetch=ids,
        inputs=[left for lefts, _ in products for left in lefts] + [right for _, right in products],
        deps=deps,
        grid=(start,),
        in_specs=in_specs,
        out_specs=[out, out],
        scratch_shapes=[pltpu.VMEM((d, tile), f32)] + [pltpu.VMEM((d, n), bf16) for _ in products],
        out_shape=[jax.ShapeDtypeStruct((count, rows, start * tile), bf16)] * 2,
        compiler_params=params(48),
        cost_estimate=cost(us),
        name="weight_grads",
    )


def last_kernel(gains, tok, mid, w_ref, *refs):
    grads, (out_ref, g_ref) = refs[:-2], refs[-2:]
    d = tok.shape[1]
    wide = grads[0].shape[2]
    dh = None
    for j, grad in enumerate(grads):
        for i in range(3):
            at = i * d + j * wide
            term = nt_dot(grad[i], w_ref[:, at : at + wide])
            dh = term if dh is None else dh + term
    scaled, inverse = norm_rows(tok[...])
    out_ref[...] = mid[...] + norm_back(dh, scaled, inverse, gains[0:1, :])

    @pl.when(pl.program_id(0) == 0)
    def _():
        g_ref[...] = jnp.zeros_like(g_ref)

    g_ref[0:1, :] += jnp.sum(dh * scaled, axis=0, keepdims=True)
    g_ref[1:2, :] += jnp.sum(dh, axis=0, keepdims=True)


def last(gains, tokens, middle_grad, dqkv, w_qkv, deps):
    n, d = tokens.shape
    tile = 256
    row = pl.BlockSpec((tile, d), lambda i: (i, 0))
    return run_kernel(
        last_kernel,
        inputs=[gains, tokens, middle_grad, w_qkv, *dqkv],
        deps=deps,
        grid=(n // tile,),
        in_specs=[
            whole(gains.shape),
            row,
            row,
            whole((d, 3 * d), 1),
        ]
        + [pl.BlockSpec((3, tile, g.shape[2]), lambda i: (0, i, 0)) for g in dqkv],
        out_specs=[row, whole((8, d))],
        out_shape=[jax.ShapeDtypeStruct((n, d), f32), jax.ShapeDtypeStruct((8, d), f32)],
        compiler_params=params(48),
        cost_estimate=cost(1),
        name="token_grads",
    )


def pick(value, index, axis):
    return lax.dynamic_index_in_dim(value, index, axis, keepdims=False)


def after(value, *others):
    for other in others:
        mark = lax.slice(other, (0,) * other.ndim, (1,) * other.ndim).reshape(()) * jnp.zeros((), other.dtype)
        value = value + mark.astype(value.dtype)
    return value


def in_order(core, mine, theirs):
    return jnp.where(core == 0, jnp.stack([mine, theirs]), jnp.stack([theirs, mine]))


def local(
    tokens,
    w_query,
    w_key,
    w_value,
    w_output,
    gain_one,
    shift_one,
    gain_two,
    shift_two,
    expert_in,
    expert_out,
    lengths,
    expert_ids,
    padding,
    cotangent,
    *,
    bits,
    fs,
):
    n, d = tokens.shape
    share, _, hidden = expert_in.shape
    owned = expert_out.shape[0]
    chips = 1 << bits
    devices = 2 * chips * fs
    hc = hidden // 2
    links = Links(bits, fs)
    core = lax.axis_index("core")
    zed = lax.axis_index("fsdp")
    chip = jnp.int32(0)
    for k in range(bits):
        chip = chip * 2 + lax.axis_index(f"b{k}")
    orders = jnp.array([[links.mask(i, c) for i in range(chips)] for c in range(2)], jnp.int32)
    near, far = chip ^ pick(orders, core, 0), chip ^ pick(orders, 1 - core, 0)
    ids = jnp.concatenate([near, near * 2 + core, far * 2 + 1 - core]).astype(jnp.int32)

    norms = jnp.stack([gain_one, shift_one, gain_two, shift_two], axis=1)
    norms = jnp.pad(norms, ((0, 0), (0, 124)))
    shard = jnp.concatenate([w_output, w_query, w_key, w_value, norms], axis=1).astype(bf16)
    line = links.gather_line(shard).reshape(fs * share, -1)

    def gather_attention(block):
        own = links.gather_chips(block)
        return own + [swap(piece, "core") for piece in own]

    pieces = gather_attention(line)

    slabs = hc // d
    in_rows, out_rows = 2 * fs * share, fs * owned
    in_low = expert_in.astype(bf16).reshape(share, 2, chips, 2, fs * owned).transpose(1, 3, 0, 2, 4)
    in_low = in_low.reshape(2, 2, share, slabs, d).transpose(0, 1, 3, 2, 4).reshape(2, -1, d)
    low = jnp.concatenate([in_low, expert_out.astype(bf16).transpose(1, 0, 2)], axis=1)
    pair = in_order(core, pick(low, core, 0), swap(pick(low, 1 - core, 0), "core"))
    in_pair = pair[:, : 2 * slabs * share].reshape(2, 2, slabs * share, d)
    out_pair = pair[:, 2 * slabs * share :]

    def gather_experts(j, before, gate):
        mine = jnp.concatenate([in_pair[:, j].reshape(-1, d), out_pair[j]], axis=0)
        got = after(links.gather_line(after(mine, before)), gate)
        in_part = got[:, : 2 * slabs * share].reshape(fs, 2, slabs, share, d)
        in_part = in_part.transpose(2, 1, 0, 3, 4).reshape(slabs * in_rows, d)
        out_part = got[:, 2 * slabs * share :].reshape(out_rows, d)
        return jnp.concatenate([in_part, out_part], axis=0)

    spots = jnp.arange(n, dtype=jnp.int32)
    eight = jnp.arange(lengths.shape[1])
    ends = jnp.sum(jnp.where(eight[:, None] <= eight[None, :], lengths[0][:, None], 0), axis=0)
    segment = jnp.sum((spots[:, None] >= ends[None, :]).astype(jnp.int32), axis=1)
    key_segment = jnp.where(padding == 1, segment, -1)
    kseg = jnp.broadcast_to(key_segment[:, None], (n, 128))
    qseg = jnp.broadcast_to(segment[None, :], (8, n))
    chosen = expert_ids[:, 0]
    names = jnp.arange(2, dtype=jnp.int32)
    hot = (chosen[:, None] == names[None, :]).astype(bf16)
    before = (spots[:, None] > spots[None, :]).astype(bf16)
    place = nn_dot(before, hot).astype(jnp.int32)
    place = jnp.where(chosen == 0, place[:, 0], place[:, 1])
    slot = jnp.where(chosen == core, place, CAP + place)
    slot_row = jnp.broadcast_to(slot[None, :], (8, n))
    slot_col = jnp.broadcast_to(slot[:, None], (n, 128))

    dy_own, dy_other = pack(slot_row, cotangent)
    dys = (dy_own, swap(dy_other, "core"))
    lines = [gather_experts(0, line, pieces[1])]
    h1, qkv, w_qkv, gains = first(ids, tokens, pieces, lines[:1])

    def spread_chunk(block, hold):
        pieces = [block]
        for t in range(bits):
            if t == bits - 1:
                pieces = [after(block, pieces[-1] if hold is None else hold)] + pieces[1:]
            pieces = pieces + [links.swap(p, t) for p in pieces]
        return [block] + pieces[1:]

    chunks = [spread_chunk(lines[0], h1)]
    lines.append(gather_experts(1, lines[0], h1))
    mixed, lse = [], []
    for i in range(PARTS):
        needs = [*lse[-1:], *chunks[0][2:-1], lines[1]] if i else [chunks[0][1]]
        made = attend(kseg, qseg, qkv, i, PARTS, needs)
        mixed.append(made[0])
        lse.append(made[1])
    chunks.append(spread_chunk(lines[1], None))
    middle, w_out, x_own, x_other = second(
        ids, slot_row, mixed, tokens, gains, pieces, []
    )
    xs = (x_own, swap(x_other, "core"))

    def line_rows(total):
        in_part = total[: slabs * in_rows].reshape(slabs, 2, fs, share, d)
        in_part = in_part.transpose(2, 1, 0, 3, 4).reshape(fs, 2 * slabs * share, d)
        return jnp.concatenate([in_part, total[slabs * in_rows :].reshape(fs, owned, d)], axis=1)

    def chip_sum(keep, send, gate):
        got = links.swap(send, bits - 1)
        for t in reversed(range(bits - 1)):
            top = keep.shape[0] // 2
            send = add_low(keep[top:], got[top:])
            total = keep[:top].astype(f32) + got[:top].astype(f32)
            first_send.append(send)
            got = links.swap(send, t)
            if t:
                keep = total.astype(bf16)
            else:
                return after((total + got.astype(f32)).astype(bf16)[0], *gate)
        return after(add_low(keep[0], got[0]), *gate)

    half = chips // 2
    near, far, keep_a, send_a = expert(ids, xs, dys, None, chunks[0], in_rows, out_rows, [chunks[1][1]])
    near, far, keep_b, send_b = expert(ids, xs, dys, [near, far], chunks[1], in_rows, out_rows, [])
    returned = (near, swap(far, "core"))

    first_send = []
    chunk_a = chip_sum(keep_a, send_a, [])
    output, grad_middle, dz, grad_mixed, sums_two, send_b = third(
        slot_col, gains, middle, cotangent, w_out, returned, first_send, [send_b]
    )

    def core_sum(made):
        return add_low(made[0], swap(made[1], "core"))

    def split_sum(total):
        got = links.swap(total[half:], bits - 1)
        return add_low(total[:half], got)

    def rest_sum(total):
        if bits > 1:
            top = total.shape[0] // 2
            total = links.reduce_chips(total[:top], total[top:], bits - 1)
        else:
            total = total[0]
        return total.reshape(fs, share, -1)

    wide = d // PARTS
    chunk_a = line_rows(after(chunk_a, dz))
    line_a = links.reduce_line(chunk_a)
    grads = [attend_back(kseg, qseg, qkv, grad_mixed, lse[0], 0, PARTS, [chunk_a])]
    made_a = weights(ids, [(mixed, dz[None]), ([h1], grads[0])], chips, 0.1)
    first_send = []
    chunk_b = chip_sum(keep_b, send_b, [])
    grads.append(
        attend_back(kseg, qseg, qkv, grad_mixed, lse[1], 1, PARTS, [made_a[1], *first_send])
    )
    chunk_b = line_rows(after(chunk_b, grads[1]))
    line_b = links.reduce_line(chunk_b)
    core_a = after(core_sum(made_a), grads[1])
    made_b = weights(ids, [([h1], grads[1])], chips, 0.1, [core_a, chunk_b])
    core_b = core_sum(made_b)
    split_a, split_b = split_sum(core_a), split_sum(core_b)
    ready = [rest_sum(split_a), rest_sum(split_b)]
    grad_tokens, sums_one = last(gains, tokens, grad_middle, grads, w_qkv, [core_b])
    ready = links.reduce_line_direct(after(jnp.concatenate(ready, axis=2), line_b), zed)
    grad_output = ready[:, :d]
    grad_qkv = [
        jnp.concatenate(
            [ready[:, d + (3 * j + i) * wide : d + (3 * j + i + 1) * wide] for j in range(PARTS)],
            axis=1,
        )
        for i in range(3)
    ]

    ins = jnp.stack([t[: 2 * slabs * share].reshape(2, slabs * share, d) for t in (line_a, line_b)])
    outs = jnp.stack([t[2 * slabs * share :] for t in (line_a, line_b)])
    theirs = jnp.concatenate([pick(ins, 1 - core, 1).reshape(-1, d), pick(outs, 1 - core, 0)], axis=0)
    got = swap(theirs, "core")
    in_grad = in_order(core, pick(ins, core, 1).reshape(-1, d), got[: 2 * slabs * share])
    in_grad = in_grad.reshape(2, 2, slabs, share, d // (fs * owned), fs * owned)
    grad_expert_in = in_grad.transpose(3, 0, 2, 4, 1, 5).reshape(share, 2, hidden)
    out_grad = in_order(core, pick(outs, core, 0), got[2 * slabs * share :])
    grad_expert_out = out_grad.transpose(1, 0, 2)

    sums = jnp.concatenate([sums_one[:2], sums_two[:2]]).reshape(4, devices, share).transpose(1, 0, 2)
    sums = after(sums, line_b)
    sums = jnp.sum(lax.all_to_all(sums, links.axes + ("fsdp",), 0, 0), axis=0)

    return (
        output,
        grad_tokens,
        grad_qkv[0],
        grad_qkv[1],
        grad_qkv[2],
        grad_output,
        sums[0],
        sums[1],
        sums[2],
        sums[3],
        grad_expert_in,
        grad_expert_out,
    )


def solution(mesh):
    dp, fs = mesh.shape["dp"], mesh.shape["fsdp"]
    bits = (dp // 2).bit_length() - 1
    names = tuple(f"b{k}" for k in range(bits)) + ("core", "fsdp")
    fine = Mesh(mesh.devices.reshape((2,) * (bits + 1) + (fs,)), names)
    rows = lambda rank: P(names, *([None] * (rank - 1)))
    in_specs = tuple(rows(r) for r in (2, 2, 2, 2, 2, 1, 1, 1, 1, 3, 3, 2, 2, 1, 2))
    out_specs = tuple(rows(r) for r in (2, 2, 2, 2, 2, 2, 1, 1, 1, 1, 3, 3))
    return jax.shard_map(
        functools.partial(local, bits=bits, fs=fs),
        mesh=fine,
        in_specs=in_specs,
        out_specs=out_specs,
        check_vma=False,
    )
```

```python
import functools
import math

import jax
import jax.numpy as jnp
from jax import lax
from jax.experimental import pallas as pl
from jax.experimental.pallas import tpu as pltpu
from jax.sharding import Mesh
from jax.sharding import PartitionSpec as P

HEADS = 16
HEAD_DIM = 64
CAP = 640
PARTS = 2
MIB = 1 << 20

norm_eps = 1e-05
neg_large = -1e30
gelu_c = math.sqrt(2.0 / math.pi)
gelu_k = 0.044715
f32 = jnp.float32
bf16 = jnp.bfloat16


def nt_dot(a, b):
    return lax.dot_general(a, b, (((1,), (1,)), ((), ())), preferred_element_type=f32)


def tn_dot(a, b):
    return lax.dot_general(a, b, (((0,), (0,)), ((), ())), preferred_element_type=f32)


def nn_dot(a, b):
    return jnp.dot(a, b, preferred_element_type=f32)


def params(mib, steps=1):
    return pltpu.CompilerParams(
        vmem_limit_bytes=mib * MIB, dimension_semantics=("arbitrary",) * steps
    )


def cost(us):
    return pl.CostEstimate(flops=int(us * 1.15e9), bytes_accessed=MIB, transcendentals=0)


def whole(shape, buffers=None):
    zeros = (0,) * len(shape)
    if buffers is None:
        return pl.BlockSpec(shape, lambda *_: zeros)
    return pl.BlockSpec(shape, lambda *_: zeros, pipeline_mode=pl.Buffered(buffers))


def run_kernel(
    kernel, *, in_specs, inputs, out_specs, out_shape, deps=(), through=(), prefetch=None, grid=(), scratch_shapes=(), **rest
):
    first_args = [] if prefetch is None else [prefetch]
    deps, through = list(deps), list(through)
    out_specs = list(out_specs) if isinstance(out_specs, (list, tuple)) else [out_specs]
    out_shape = list(out_shape) if isinstance(out_shape, (list, tuple)) else [out_shape]
    a = len(first_args) + len(inputs)
    b = a + len(deps) + len(through)
    c = b + len(out_shape)

    def body(*refs):
        kernel(*refs[:a], *refs[b:c], *refs[c + len(through) :])

    far = pl.BlockSpec(memory_space=pl.ANY)
    spec = pltpu.PrefetchScalarGridSpec(
        num_scalar_prefetch=len(first_args),
        grid=grid,
        in_specs=list(in_specs) + [far] * (b - a),
        out_specs=out_specs + [far] * len(through),
        scratch_shapes=list(scratch_shapes),
    )
    made = pl.pallas_call(
        body,
        grid_spec=spec,
        out_shape=out_shape + [jax.ShapeDtypeStruct(t.shape, t.dtype) for t in through],
        input_output_aliases={a + len(deps) + i: len(out_shape) + i for i in range(len(through))},
        **rest,
    )(*first_args, *inputs, *deps, *through)
    return made if len(made) > 1 else made[0]


def swap(value, axis):
    return lax.ppermute(value, axis, [(0, 1), (1, 0)])


class Links:
    def __init__(self, bits, fs):
        self.bits = bits
        self.fs = fs
        self.axes = tuple(f"b{k}" for k in range(bits)) + ("core",)

    def axis(self, step, core):
        return (step + core) % self.bits

    def flip(self, step, core):
        return 1 << (self.bits - 1 - self.axis(step, core))

    def mask(self, index, core):
        return sum(self.flip(t, core) for t in range(self.bits) if index >> t & 1)

    def swap(self, value, step):
        pairs = []
        for source in range(2 << self.bits):
            core = source & 1
            pairs.append((source, source ^ (self.flip(step, core) << 1)))
        return lax.ppermute(value, self.axes, pairs)

    def gather_line(self, shard):
        spread = jnp.broadcast_to(shard[None], (self.fs,) + shard.shape)
        return lax.all_to_all(spread, "fsdp", 0, 0)

    def gather_chips(self, block):
        pieces = [block]
        for t in range(self.bits):
            pieces = pieces + [self.swap(p, t) for p in pieces]
        return pieces

    def reduce_chips(self, keep, send, steps):
        for t in reversed(range(steps)):
            got = self.swap(send, t)
            if t > 0:
                half = keep.shape[0] // 2
                send = add_low(keep[half:], got[half:])
                keep = add_low(keep[:half], got[:half])
            else:
                keep = add_low(keep[0], got[0])
        return keep

    def reduce_line_direct(self, value, zed, hold):
        total = after(pick(value, zed, 0).astype(f32), *hold)
        for t in range(1, self.fs):
            pairs = [(z, (z + t) % self.fs) for z in range(self.fs)]
            part = lax.ppermute(pick(value, (zed + t) % self.fs, 0), "fsdp", pairs)
            total = total + part.astype(f32)
        return total

    def reduce_line(self, value):
        got = lax.all_to_all(value, "fsdp", 0, 0)
        return jnp.sum(got.astype(f32), axis=0)


def add_low(a, b):
    return (a.astype(f32) + b.astype(f32)).astype(bf16)


def norm_rows(values):
    center = values - jnp.mean(values, axis=1, keepdims=True)
    inverse = lax.rsqrt(jnp.mean(center * center, axis=1, keepdims=True) + norm_eps)
    return center * inverse, inverse


def norm_back(grad_rows, scaled, inverse, gain):
    inner = grad_rows * gain
    return inverse * (
        inner
        - jnp.mean(inner, axis=1, keepdims=True)
        - scaled * jnp.mean(inner * scaled, axis=1, keepdims=True)
    )


def load_rows(ids, pieces, rows, store):
    for i, piece in enumerate(pieces):
        store(pl.multiple_of(ids[len(pieces) // 2 + i] * rows, rows), piece)


def first_kernel(ids, tok, *refs, count, rows, width):
    pieces = refs[:count]
    h_ref, qkv_ref, w_ref, g_ref, norms = refs[count:]

    @pl.when(pl.program_id(0) == 0)
    def _():
        def store(at, piece):
            w_ref[pl.ds(at, rows), :] = piece[:, width : 4 * width]
            norms[pl.ds(at, rows), :] = piece[:, 4 * width :].astype(f32)

        load_rows(ids, pieces, rows, store)
        g_ref[...] = jnp.transpose(norms[...])[:8]

    scaled, _ = norm_rows(tok[...])
    h = (scaled * g_ref[0:1, :] + g_ref[1:2, :]).astype(bf16)
    h_ref[...] = h
    for i in range(3):
        out = nn_dot(h, w_ref[:, i * width : (i + 1) * width]).astype(bf16)
        if i == 0:
            out = out * jnp.asarray(1.0 / math.sqrt(HEAD_DIM), bf16)
        qkv_ref[i] = out


def first(ids, tokens, pieces, deps):
    n, d = tokens.shape
    rows, cols = pieces[0].shape
    tile = 256
    return run_kernel(
        functools.partial(first_kernel, count=len(pieces), rows=rows, width=d),
        prefetch=ids,
        inputs=[tokens, *pieces],
        deps=deps,
        grid=(n // tile,),
        in_specs=[pl.BlockSpec((tile, d), lambda i, s: (i, 0))]
        + [whole((rows, cols), 1) for _ in pieces],
        out_specs=[
            pl.BlockSpec((tile, d), lambda i, s: (i, 0)),
            pl.BlockSpec((3, tile, d), lambda i, s: (0, i, 0)),
            whole((d, 3 * d)),
            whole((8, d)),
        ],
        scratch_shapes=[pltpu.VMEM((d, 128), f32)],
        out_shape=[
            jax.ShapeDtypeStruct((n, d), bf16),
            jax.ShapeDtypeStruct((3, n, d), bf16),
            jax.ShapeDtypeStruct((d, 3 * d), bf16),
            jax.ShapeDtypeStruct((8, d), f32),
        ],
        compiler_params=params(56),
        cost_estimate=cost(16),
        name="qkv",
    )


def make_bias(bias, kseg, qseg, n):
    key_at = lax.broadcasted_iota(jnp.int32, (256, n), 0)
    query_at = lax.broadcasted_iota(jnp.int32, (256, n), 1)
    for b in range(n // 256):
        rows = key_at + b * 256
        same = kseg[b * 256 : (b + 1) * 256, 0:1] == qseg[0:1, :]
        seen = (same & (rows <= query_at)) | (rows == query_at)
        bias[b * 256 : (b + 1) * 256, :] = jnp.where(seen, 0.0, neg_large)


def head_mask(block, head):
    lane = lax.broadcasted_iota(jnp.int32, block.shape, 1)
    return jnp.where((lane < HEAD_DIM) == (head == 0), block, jnp.zeros_like(block))


def attend_kernel(kseg, qseg, qkv, o_ref, lse_ref, bias, *, n):
    @pl.when(pl.program_id(0) == 0)
    def _():
        make_bias(bias, kseg, qseg, n)

    k = qkv[1]
    v_t = jnp.transpose(qkv[2])
    for i in range(n // 256):
        keys = (i + 1) * 256
        cols = slice(i * 256, keys)
        q = qkv[0, cols, :]
        parts = []
        for head in range(2):
            s = nt_dot(k[:keys], head_mask(q, head)) + bias[:keys, cols]
            peak = jnp.max(s, axis=0, keepdims=True)
            e = jnp.exp(s - peak)
            total = jnp.sum(e, axis=0, keepdims=True)
            p = (e * (1.0 / total)).astype(bf16)
            parts.append(nn_dot(v_t[head * HEAD_DIM : (head + 1) * HEAD_DIM, :keys], p))
            lse_ref[0, head : head + 1, cols] = peak + jnp.log(total)
        o_ref[cols, :] = jnp.transpose(jnp.concatenate(parts, axis=0)).astype(bf16)


def attend(kseg, qseg, qkv, part, parts, deps):
    _, n, d = qkv.shape
    pairs = d // 128 // parts
    d = d // parts
    return run_kernel(
        functools.partial(attend_kernel, n=n),
        inputs=[kseg, qseg, qkv],
        deps=deps,
        grid=(pairs,),
        in_specs=[
            whole(kseg.shape),
            whole(qseg.shape),
            pl.BlockSpec((3, n, 128), lambda p: (0, 0, p + part * pairs)),
        ],
        out_specs=[
            pl.BlockSpec((n, 128), lambda p: (0, p)),
            pl.BlockSpec((1, 8, n), lambda p: (p, 0, 0)),
        ],
        out_shape=[
            jax.ShapeDtypeStruct((n, d), bf16),
            jax.ShapeDtypeStruct((pairs, 8, n), f32),
        ],
        scratch_shapes=[pltpu.VMEM((n, n), f32)],
        compiler_params=params(48),
        cost_estimate=cost(21),
        name="attend",
    )


def attend_back_kernel(kseg, qseg, qkv, do_ref, lse_ref, out, bias, dk_acc, dv_acc, *, n):
    @pl.when(pl.program_id(0) == 0)
    def _():
        make_bias(bias, kseg, qseg, n)

    k = qkv[1]
    v = qkv[2]
    k_t = jnp.transpose(k)
    blocks = n // 256
    for i in reversed(range(blocks)):
        keys = (i + 1) * 256
        cols = slice(i * 256, keys)
        parts = []
        for head in range(2):
            q = head_mask(qkv[0, cols, :], head)
            go = head_mask(do_ref[cols, :], head)
            s = nt_dot(k[:keys], q) + bias[:keys, cols]
            p = jnp.exp(s - lse_ref[0, head : head + 1, cols])
            dp = nt_dot(v[:keys], go)
            inner = jnp.sum(p * dp, axis=0, keepdims=True)
            ds = (p * (dp - inner)).astype(bf16)
            dv = nn_dot(p.astype(bf16), go)
            dk = nn_dot(ds, q)
            if i == blocks - 1 and head == 0:
                dv_acc[...] = dv
                dk_acc[...] = dk
            else:
                dv_acc[:keys, :] += dv
                dk_acc[:keys, :] += dk
            parts.append(nn_dot(k_t[head * HEAD_DIM : (head + 1) * HEAD_DIM, :keys], ds))
        dq = jnp.concatenate(parts, axis=0) * (1.0 / math.sqrt(HEAD_DIM))
        out[0, cols, :] = jnp.transpose(dq).astype(bf16)
    out[1] = dk_acc[...].astype(bf16)
    out[2] = dv_acc[...].astype(bf16)


def attend_back(kseg, qseg, qkv, grad_mixed, lse, part, parts, deps):
    _, n, d = qkv.shape
    pairs = d // 128 // parts
    d = d // parts
    return run_kernel(
        functools.partial(attend_back_kernel, n=n),
        inputs=[kseg, qseg, qkv, grad_mixed, lse],
        deps=deps,
        grid=(pairs,),
        in_specs=[
            whole(kseg.shape),
            whole(qseg.shape),
            pl.BlockSpec((3, n, 128), lambda p: (0, 0, p + part * pairs)),
            pl.BlockSpec((n, 128), lambda p: (0, p + part * pairs)),
            pl.BlockSpec((1, 8, n), lambda p: (p, 0, 0)),
        ],
        out_specs=pl.BlockSpec((3, n, 128), lambda p: (0, 0, p)),
        out_shape=jax.ShapeDtypeStruct((3, n, d), bf16),
        scratch_shapes=[
            pltpu.VMEM((n, n), f32),
            pltpu.VMEM((n, 128), f32),
            pltpu.VMEM((n, 128), f32),
        ],
        compiler_params=params(56),
        cost_estimate=cost(22),
        name="attend_back",
    )


def slot_hot(slot_row, start, count):
    n = slot_row.shape[1]
    at = lax.broadcasted_iota(jnp.int32, (count, n), 0) + start
    return jnp.where(at == slot_row, 1.0, 0.0).astype(bf16)


def pack_kernel(slot_row, values, own, other):
    low = values[...].astype(bf16)
    own[...] = nn_dot(slot_hot(slot_row[0:1, :], 0, CAP), low).astype(bf16)
    other[...] = nn_dot(slot_hot(slot_row[0:1, :], CAP, CAP), low).astype(bf16)


def pack(slot_row, values):
    n, d = values.shape
    return pl.pallas_call(
        pack_kernel,
        in_specs=[whole(slot_row.shape), whole((n, d))],
        out_specs=[whole((CAP, d))] * 2,
        out_shape=[jax.ShapeDtypeStruct((CAP, d), bf16)] * 2,
        compiler_params=pltpu.CompilerParams(vmem_limit_bytes=48 * MIB),
        cost_estimate=cost(0.1),
        name="pack",
    )(slot_row, values)


def second_kernel(ids, slot_row, tok, gains, *refs, count, rows, steps, tile, parts):
    mixed, refs = refs[:parts], refs[parts:]
    pieces = refs[:count]
    x_ref, w_ref, own, other, h_all = refs[count:]
    step = pl.program_id(0)

    @pl.when(step == 0)
    def _():
        def store(at, piece):
            w_ref[pl.ds(at, rows), :] = piece[...]

        load_rows(ids, pieces, rows, store)

    x = tok[...]
    wide = mixed[0].shape[1]
    for i, o_ref in enumerate(mixed):
        x = x + nn_dot(o_ref[...], w_ref[i * wide : (i + 1) * wide, :])
    x_ref[...] = x
    scaled, _ = norm_rows(x)
    h = (scaled * gains[2:3, :] + gains[3:4, :]).astype(bf16)
    h_all[pl.ds(pl.multiple_of(step * tile, tile), tile), :] = h

    @pl.when(step == steps - 1)
    def _():
        own[...] = nn_dot(slot_hot(slot_row[0:1, :], 0, CAP), h_all[...]).astype(bf16)
        other[...] = nn_dot(slot_hot(slot_row[0:1, :], CAP, CAP), h_all[...]).astype(bf16)


def second(ids, slot_row, mixed, tokens, gains, pieces, deps):
    n, d = tokens.shape
    rows = pieces[0].shape[0]
    tile = 256
    return run_kernel(
        functools.partial(
            second_kernel, count=len(pieces), rows=rows, steps=n // tile, tile=tile, parts=len(mixed)
        ),
        prefetch=ids,
        inputs=[slot_row, tokens, gains, *mixed, *pieces],
        deps=deps,
        **dict(
            grid=(n // tile,),
            in_specs=[
                whole(slot_row.shape),
                pl.BlockSpec((tile, d), lambda i, s: (i, 0)),
                whole(gains.shape),
            ]
            + [pl.BlockSpec((tile, o.shape[1]), lambda i, s: (i, 0)) for o in mixed]
            + [whole((rows, d), 1) for _ in pieces],
            out_specs=[
                pl.BlockSpec((tile, d), lambda i, s: (i, 0)),
                whole((d, d)),
                whole((CAP, d)),
                whole((CAP, d)),
            ],
            scratch_shapes=[pltpu.VMEM((n, d), bf16)],
        ),
        out_shape=[
            jax.ShapeDtypeStruct((n, d), f32),
            jax.ShapeDtypeStruct((d, d), bf16),
            jax.ShapeDtypeStruct((CAP, d), bf16),
            jax.ShapeDtypeStruct((CAP, d), bf16),
        ],
        compiler_params=params(56),
        cost_estimate=cost(1),
        name="mix_out",
    )


def expert_kernel(ids, *refs, count, rows, tile, first_chunk, block):
    xs, ys = refs[0:2], refs[2:4]
    pos = 4
    prior = None
    if not first_chunk:
        prior = refs[pos : pos + 2]
        pos += 2
    pieces = refs[pos : pos + count]
    pos += count
    near, far, keep, send = refs[pos : pos + 4]
    x_s, dy_s, win_s, wout_s, y_acc, h_acc, a_s, du_s, sems = refs[pos + 4 :]
    half = count // 2
    step = pl.program_id(0)
    d = x_s.shape[1]
    slabs = win_s.shape[1] // d
    total = 2 * CAP

    @pl.when(step == 0)
    def _():
        copies = []

        def fetch(source, target):
            copy = pltpu.make_async_copy(source, target, sems.at[len(copies)])
            copy.start()
            copies.append(copy)

        for side in range(2):
            fetch(xs[side], x_s.at[pl.ds(side * CAP, CAP)])
        for i in range(count):
            at = pl.multiple_of(ids[i] * rows, rows)
            for h in range(slabs):
                fetch(
                    pieces[i].at[pl.ds(h * rows, rows)],
                    win_s.at[pl.ds(at, rows), pl.ds(h * d, d)],
                )
        for side in range(2):
            fetch(ys[side], dy_s.at[pl.ds(side * CAP, CAP)])
        for i in range(count):
            at = pl.multiple_of(ids[i] * tile, tile)
            fetch(pieces[i].at[pl.ds(slabs * rows, tile)], wout_s.at[pl.ds(at, tile)])
        if first_chunk:
            y_acc[...] = jnp.zeros_like(y_acc)
            h_acc[...] = jnp.zeros_like(h_acc)
        else:
            for side in range(2):
                span = slice(side * CAP, (side + 1) * CAP)
                y_acc[span, :] = prior[side][0].astype(f32)
                h_acc[span, :] = prior[side][1].astype(f32)
        for copy in copies:
            copy.wait()

    at = pl.multiple_of(ids[step] * tile, tile)

    def one_block(b, carry):
        span = pl.ds(pl.multiple_of(b * block, block), block)
        u = nn_dot(x_s[span, :], win_s[:, pl.ds(at, tile)])
        da = nt_dot(dy_s[span, :], wout_s[pl.ds(at, tile), :])
        square = u * u
        t = jnp.tanh(gelu_c * (u * (1.0 + gelu_k * square)))
        up = 0.5 * (1.0 + t)
        slope = up + (0.5 * gelu_c) * u * (1.0 - t * t) * (1.0 + 3.0 * gelu_k * square)
        a = (u * up).astype(bf16)
        du = (da * slope).astype(bf16)
        a_s[span, :] = a
        du_s[span, :] = du
        y_acc[span, :] += nn_dot(a, wout_s[pl.ds(at, tile), :])
        h_acc[span, :] += nt_dot(du, win_s[:, pl.ds(at, tile)])
        return carry

    lax.fori_loop(0, total // block, one_block, 0, unroll=True)
    grad = tn_dot(a_s[...], dy_s[...]).astype(bf16)

    for i in range(count):

        @pl.when(step == i)
        def _():
            (keep if i < half else send)[i % half, slabs * rows :, :] = grad

    slab = at // d
    row = pl.multiple_of(slab * rows, rows)
    col = pl.multiple_of(at - slab * d, tile)

    for i in range(count):
        src = pl.multiple_of(ids[i] * rows, rows)
        (keep if i < half else send)[i % half, pl.ds(row, rows), pl.ds(col, tile)] = tn_dot(
            x_s[:, pl.ds(src, rows)], du_s[...]
        ).astype(bf16)

    @pl.when(step == count - 1)
    def _():
        for side in range(2):
            span = slice(side * CAP, (side + 1) * CAP)
            (near, far)[side][0] = y_acc[span, :].astype(bf16)
            (near, far)[side][1] = h_acc[span, :].astype(bf16)


def expert(ids, xs, ys, prior, pieces, rows, tile, deps):
    count = len(pieces)
    d = xs[0].shape[1]
    hc = count * tile
    total = 2 * CAP
    first_chunk = prior is None
    far = pl.BlockSpec(memory_space=pl.ANY)
    part = (count // 2,) + pieces[0].shape
    return run_kernel(
        functools.partial(
            expert_kernel, count=count, rows=rows, tile=tile, first_chunk=first_chunk, block=320
        ),
        prefetch=ids,
        inputs=list(xs) + list(ys) + list(prior or ()) + list(pieces),
        deps=deps,
        grid=(count,),
        in_specs=[far] * 4
        + ([] if first_chunk else [whole((2, CAP, d), 1)] * 2)
        + [far] * count,
        out_specs=[whole((2, CAP, d), 1)] * 2 + [whole(part, 1)] * 2,
        scratch_shapes=[
            pltpu.VMEM((total, d), bf16),
            pltpu.VMEM((total, d), bf16),
            pltpu.VMEM((d, hc), bf16),
            pltpu.VMEM((hc, d), bf16),
            pltpu.VMEM((total, d), f32),
            pltpu.VMEM((total, d), f32),
            pltpu.VMEM((total, tile), bf16),
            pltpu.VMEM((total, tile), bf16),
            pltpu.SemaphoreType.DMA((4 + (hc // d + 1) * count,)),
        ],
        out_shape=[jax.ShapeDtypeStruct((2, CAP, d), bf16)] * 2
        + [jax.ShapeDtypeStruct(part, bf16)] * 2,
        compiler_params=params(60),
        cost_estimate=cost(53),
        name="experts",
    )


def third_kernel(slot_col, gains, x_ref, cot, w_ref, *refs):
    near, far, out_ref, mid_ref, dz_ref, do_ref, g_ref = refs
    tile = x_ref.shape[0]
    at = lax.broadcasted_iota(jnp.int32, (tile, CAP), 1)
    own = jnp.where(slot_col[:, 0:1] == at, 1.0, 0.0).astype(bf16)
    other = jnp.where(slot_col[:, 0:1] == at + CAP, 1.0, 0.0).astype(bf16)
    x = x_ref[...]
    out_ref[...] = x + nn_dot(own, near[0]) + nn_dot(other, far[0])
    dh = nn_dot(own, near[1]) + nn_dot(other, far[1])
    scaled, inverse = norm_rows(x)
    mid = cot[...] + norm_back(dh, scaled, inverse, gains[2:3, :])
    mid_ref[...] = mid
    dz = mid.astype(bf16)
    dz_ref[...] = dz
    do_ref[...] = nt_dot(dz, w_ref[...]).astype(bf16)

    @pl.when(pl.program_id(0) == 0)
    def _():
        g_ref[...] = jnp.zeros_like(g_ref)

    g_ref[0:1, :] += jnp.sum(dh * scaled, axis=0, keepdims=True)
    g_ref[1:2, :] += jnp.sum(dh, axis=0, keepdims=True)


def third(slot_col, gains, middle, cot, w_out, returned, deps, through):
    n, d = middle.shape
    tile = 256
    row = pl.BlockSpec((tile, d), lambda i: (i, 0))
    return run_kernel(
        third_kernel,
        inputs=[slot_col, gains, middle, cot, w_out, *returned],
        deps=deps,
        through=through,
        grid=(n // tile,),
        in_specs=[
            pl.BlockSpec((tile, slot_col.shape[1]), lambda i: (i, 0)),
            whole(gains.shape),
            row,
            row,
            whole((d, d), 1),
        ]
        + [whole((2, CAP, d), 1)] * 2,
        out_specs=[row, row, row, row, whole((8, d))],
        out_shape=[
            jax.ShapeDtypeStruct((n, d), f32),
            jax.ShapeDtypeStruct((n, d), f32),
            jax.ShapeDtypeStruct((n, d), bf16),
            jax.ShapeDtypeStruct((n, d), bf16),
            jax.ShapeDtypeStruct((8, d), f32),
        ],
        compiler_params=params(56),
        cost_estimate=cost(17),
        name="combine",
    )


def weights_kernel(ids, *refs, count, rows, groups, steps):
    total = sum(groups)
    lefts, rights = refs[:total], refs[total : total + len(groups)]
    keep, send, res, *turned = refs[total + len(groups) :]
    step = pl.program_id(0)

    @pl.when(step == 0)
    def _():
        k = 0
        for size, left_t in zip(groups, turned):
            wide = lefts[k].shape[1]
            for i in range(size):
                left_t[i * wide : (i + 1) * wide, :] = jnp.transpose(lefts[k + i][...])
            k += size

    start = 0
    for right, left_t, size in zip(rights, turned, steps):

        @pl.when((step >= start) & (step < start + size))
        def _():
            res[...] = nn_dot(left_t[...], right[0])

        start += size
    for i in range(count):
        for out, r in ((keep, count + i), (send, 2 * count + i)):
            src = pl.multiple_of(ids[r] * rows, rows)
            out[i] = res[pl.ds(src, rows), :].astype(bf16)


def weights(ids, products, count, us, deps=(), tile=512):
    n = products[0][1].shape[1]
    d = sum(left.shape[1] for left in products[0][0])
    rows = d // (2 * count)
    steps = [right.shape[0] * right.shape[2] // tile for _, right in products]
    in_specs = [whole(left.shape, 1) for lefts, _ in products for left in lefts]
    start = 0
    for (_, right), size in zip(products, steps):
        per = right.shape[2] // tile

        def place(j, s, start=start, size=size, per=per):
            at = jnp.clip(j - start, 0, size - 1)
            return at // per, 0, at % per

        in_specs.append(pl.BlockSpec((1, n, tile), place))
        start += size
    out = pl.BlockSpec((count, rows, tile), lambda j, s: (0, 0, j))
    return run_kernel(
        functools.partial(
            weights_kernel,
            count=count,
            rows=rows,
            groups=[len(lefts) for lefts, _ in products],
            steps=steps,
        ),
        prefetch=ids,
        inputs=[left for lefts, _ in products for left in lefts] + [right for _, right in products],
        deps=deps,
        grid=(start,),
        in_specs=in_specs,
        out_specs=[out, out],
        scratch_shapes=[pltpu.VMEM((d, tile), f32)] + [pltpu.VMEM((d, n), bf16) for _ in products],
        out_shape=[jax.ShapeDtypeStruct((count, rows, start * tile), bf16)] * 2,
        compiler_params=params(48),
        cost_estimate=cost(us),
        name="weight_grads",
    )


def last_kernel(gains, tok, mid, w_ref, *refs):
    grads, (out_ref, g_ref) = refs[:-2], refs[-2:]
    d = tok.shape[1]
    wide = grads[0].shape[2]
    dh = None
    for j, grad in enumerate(grads):
        for i in range(3):
            at = i * d + j * wide
            term = nt_dot(grad[i], w_ref[:, at : at + wide])
            dh = term if dh is None else dh + term
    scaled, inverse = norm_rows(tok[...])
    out_ref[...] = mid[...] + norm_back(dh, scaled, inverse, gains[0:1, :])

    @pl.when(pl.program_id(0) == 0)
    def _():
        g_ref[...] = jnp.zeros_like(g_ref)

    g_ref[0:1, :] += jnp.sum(dh * scaled, axis=0, keepdims=True)
    g_ref[1:2, :] += jnp.sum(dh, axis=0, keepdims=True)


def last(gains, tokens, middle_grad, dqkv, w_qkv, deps):
    n, d = tokens.shape
    tile = 256
    row = pl.BlockSpec((tile, d), lambda i: (i, 0))
    return run_kernel(
        last_kernel,
        inputs=[gains, tokens, middle_grad, w_qkv, *dqkv],
        deps=deps,
        grid=(n // tile,),
        in_specs=[
            whole(gains.shape),
            row,
            row,
            whole((d, 3 * d), 1),
        ]
        + [pl.BlockSpec((3, tile, g.shape[2]), lambda i: (0, i, 0)) for g in dqkv],
        out_specs=[row, whole((8, d))],
        out_shape=[jax.ShapeDtypeStruct((n, d), f32), jax.ShapeDtypeStruct((8, d), f32)],
        compiler_params=params(48),
        cost_estimate=cost(1),
        name="token_grads",
    )


def pick(value, index, axis):
    return lax.dynamic_index_in_dim(value, index, axis, keepdims=False)


def after(value, *others):
    for other in others:
        mark = lax.slice(other, (0,) * other.ndim, (1,) * other.ndim).reshape(()) * jnp.zeros((), other.dtype)
        value = value + mark.astype(value.dtype)
    return value


def in_order(core, mine, theirs):
    return jnp.where(core == 0, jnp.stack([mine, theirs]), jnp.stack([theirs, mine]))


def local(
    tokens,
    w_query,
    w_key,
    w_value,
    w_output,
    gain_one,
    shift_one,
    gain_two,
    shift_two,
    expert_in,
    expert_out,
    lengths,
    expert_ids,
    padding,
    cotangent,
    *,
    bits,
    fs,
):
    n, d = tokens.shape
    share, _, hidden = expert_in.shape
    owned = expert_out.shape[0]
    chips = 1 << bits
    devices = 2 * chips * fs
    hc = hidden // 2
    links = Links(bits, fs)
    core = lax.axis_index("core")
    zed = lax.axis_index("fsdp")
    chip = jnp.int32(0)
    for k in range(bits):
        chip = chip * 2 + lax.axis_index(f"b{k}")
    orders = jnp.array([[links.mask(i, c) for i in range(chips)] for c in range(2)], jnp.int32)
    near, far = chip ^ pick(orders, core, 0), chip ^ pick(orders, 1 - core, 0)
    ids = jnp.concatenate([near, near * 2 + core, far * 2 + 1 - core]).astype(jnp.int32)

    norms = jnp.stack([gain_one, shift_one, gain_two, shift_two], axis=1)
    norms = jnp.pad(norms, ((0, 0), (0, 124)))
    shard = jnp.concatenate([w_output, w_query, w_key, w_value, norms], axis=1).astype(bf16)
    line = links.gather_line(shard).reshape(fs * share, -1)

    def gather_attention(block):
        own = links.gather_chips(block)
        return own + [swap(piece, "core") for piece in own]

    pieces = gather_attention(line)

    slabs = hc // d
    in_rows, out_rows = 2 * fs * share, fs * owned
    in_low = expert_in.astype(bf16).reshape(share, 2, chips, 2, fs * owned).transpose(1, 3, 0, 2, 4)
    in_low = in_low.reshape(2, 2, share, slabs, d).transpose(0, 1, 3, 2, 4).reshape(2, -1, d)
    low = jnp.concatenate([in_low, expert_out.astype(bf16).transpose(1, 0, 2)], axis=1)
    pair = in_order(core, pick(low, core, 0), swap(pick(low, 1 - core, 0), "core"))
    in_pair = pair[:, : 2 * slabs * share].reshape(2, 2, slabs * share, d)
    out_pair = pair[:, 2 * slabs * share :]

    def gather_experts(j, before, gate):
        mine = jnp.concatenate([in_pair[:, j].reshape(-1, d), out_pair[j]], axis=0)
        got = after(links.gather_line(after(mine, before)), gate)
        in_part = got[:, : 2 * slabs * share].reshape(fs, 2, slabs, share, d)
        in_part = in_part.transpose(2, 1, 0, 3, 4).reshape(slabs * in_rows, d)
        out_part = got[:, 2 * slabs * share :].reshape(out_rows, d)
        return jnp.concatenate([in_part, out_part], axis=0)

    spots = jnp.arange(n, dtype=jnp.int32)
    eight = jnp.arange(lengths.shape[1])
    ends = jnp.sum(jnp.where(eight[:, None] <= eight[None, :], lengths[0][:, None], 0), axis=0)
    segment = jnp.sum((spots[:, None] >= ends[None, :]).astype(jnp.int32), axis=1)
    key_segment = jnp.where(padding == 1, segment, -1)
    kseg = jnp.broadcast_to(key_segment[:, None], (n, 128))
    qseg = jnp.broadcast_to(segment[None, :], (8, n))
    chosen = expert_ids[:, 0]
    names = jnp.arange(2, dtype=jnp.int32)
    hot = (chosen[:, None] == names[None, :]).astype(bf16)
    before = (spots[:, None] > spots[None, :]).astype(bf16)
    place = nn_dot(before, hot).astype(jnp.int32)
    place = jnp.where(chosen == 0, place[:, 0], place[:, 1])
    slot = jnp.where(chosen == core, place, CAP + place)
    slot_row = jnp.broadcast_to(slot[None, :], (8, n))
    slot_col = jnp.broadcast_to(slot[:, None], (n, 128))

    dy_own, dy_other = pack(slot_row, cotangent)
    dys = (dy_own, swap(dy_other, "core"))
    lines = [gather_experts(0, line, pieces[1])]
    h1, qkv, w_qkv, gains = first(ids, tokens, pieces, lines[:1])

    def spread_chunk(block, hold):
        pieces = [block]
        for t in range(bits):
            if t == bits - 1:
                pieces = [after(block, pieces[-1] if hold is None else hold)] + pieces[1:]
            pieces = pieces + [links.swap(p, t) for p in pieces]
        return [block] + pieces[1:]

    chunks = [spread_chunk(lines[0], h1)]
    lines.append(gather_experts(1, lines[0], h1))
    mixed, lse = [], []
    for i in range(PARTS):
        needs = [*lse[-1:], *chunks[0][2:-1], lines[1]] if i else [chunks[0][1]]
        made = attend(kseg, qseg, qkv, i, PARTS, needs)
        mixed.append(made[0])
        lse.append(made[1])
    chunks.append(spread_chunk(lines[1], None))
    middle, w_out, x_own, x_other = second(
        ids, slot_row, mixed, tokens, gains, pieces, []
    )
    xs = (x_own, swap(x_other, "core"))

    def line_rows(total):
        in_part = total[: slabs * in_rows].reshape(slabs, 2, fs, share, d)
        in_part = in_part.transpose(2, 1, 0, 3, 4).reshape(fs, 2 * slabs * share, d)
        return jnp.concatenate([in_part, total[slabs * in_rows :].reshape(fs, owned, d)], axis=1)

    def chip_sum(keep, send, gate):
        got = links.swap(send, bits - 1)
        for t in reversed(range(bits - 1)):
            top = keep.shape[0] // 2
            send = add_low(keep[top:], got[top:])
            total = keep[:top].astype(f32) + got[:top].astype(f32)
            first_send.append(send)
            got = links.swap(send, t)
            if t:
                keep = total.astype(bf16)
            else:
                return after((total + got.astype(f32)).astype(bf16)[0], *gate)
        return after(add_low(keep[0], got[0]), *gate)

    half = chips // 2
    near, far, keep_a, send_a = expert(ids, xs, dys, None, chunks[0], in_rows, out_rows, [chunks[1][1]])
    near, far, keep_b, send_b = expert(ids, xs, dys, [near, far], chunks[1], in_rows, out_rows, [])
    returned = (near, swap(far, "core"))

    first_send = []
    chunk_a = chip_sum(keep_a, send_a, [])
    output, grad_middle, dz, grad_mixed, sums_two, send_b = third(
        slot_col, gains, middle, cotangent, w_out, returned, first_send, [send_b]
    )

    def core_sum(made):
        return add_low(made[0], swap(made[1], "core"))

    def split_sum(total):
        got = links.swap(total[half:], bits - 1)
        return add_low(total[:half], got)

    def rest_sum(total):
        if bits > 1:
            top = total.shape[0] // 2
            total = links.reduce_chips(total[:top], total[top:], bits - 1)
        else:
            total = total[0]
        return total.reshape(fs, share, -1)

    wide = d // PARTS
    chunk_a = line_rows(after(chunk_a, dz))
    line_a = links.reduce_line(chunk_a)
    grads = [attend_back(kseg, qseg, qkv, grad_mixed, lse[0], 0, PARTS, [chunk_a])]
    made_a = weights(ids, [(mixed, dz[None]), ([h1], grads[0])], chips, 0.1)
    first_send = []
    chunk_b = chip_sum(keep_b, send_b, [])
    grads.append(
        attend_back(kseg, qseg, qkv, grad_mixed, lse[1], 1, PARTS, [made_a[1], *first_send])
    )
    chunk_b = line_rows(after(chunk_b, grads[1]))
    line_b = links.reduce_line(chunk_b)
    core_a = after(core_sum(made_a), grads[1])
    made_b = weights(ids, [([h1], grads[1])], chips, 0.1, [core_a, chunk_b])
    core_b = core_sum(made_b)
    split_a, split_b = split_sum(core_a), after(split_sum(core_b), line_b)
    ready = [rest_sum(split_a), rest_sum(split_b)]
    grad_tokens, sums_one = last(gains, tokens, grad_middle, grads, w_qkv, [core_b])
    ins = jnp.stack([t[: 2 * slabs * share].reshape(2, slabs * share, d) for t in (line_a, line_b)])
    outs = jnp.stack([t[2 * slabs * share :] for t in (line_a, line_b)])
    theirs = jnp.concatenate([pick(ins, 1 - core, 1).reshape(-1, d), pick(outs, 1 - core, 0)], axis=0)
    got = swap(theirs, "core")
    in_grad = in_order(core, pick(ins, core, 1).reshape(-1, d), got[: 2 * slabs * share])
    in_grad = in_grad.reshape(2, 2, slabs, share, d // (fs * owned), fs * owned)
    grad_expert_in = in_grad.transpose(3, 0, 2, 4, 1, 5).reshape(share, 2, hidden)
    out_grad = in_order(core, pick(outs, core, 0), got[2 * slabs * share :])
    grad_expert_out = out_grad.transpose(1, 0, 2)

    ready = links.reduce_line_direct(jnp.concatenate(ready, axis=2), zed, [grad_expert_in, grad_expert_out])
    grad_output = ready[:, :d]
    grad_qkv = [
        jnp.concatenate(
            [ready[:, d + (3 * j + i) * wide : d + (3 * j + i + 1) * wide] for j in range(PARTS)],
            axis=1,
        )
        for i in range(3)
    ]

    sums = jnp.concatenate([sums_one[:2], sums_two[:2]]).reshape(4, devices, share).transpose(1, 0, 2)
    sums = after(sums, line_b)
    sums = jnp.sum(lax.all_to_all(sums, links.axes + ("fsdp",), 0, 0), axis=0)

    return (
        output,
        grad_tokens,
        grad_qkv[0],
        grad_qkv[1],
        grad_qkv[2],
        grad_output,
        sums[0],
        sums[1],
        sums[2],
        sums[3],
        grad_expert_in,
        grad_expert_out,
    )


def solution(mesh):
    dp, fs = mesh.shape["dp"], mesh.shape["fsdp"]
    bits = (dp // 2).bit_length() - 1
    names = tuple(f"b{k}" for k in range(bits)) + ("core", "fsdp")
    fine = Mesh(mesh.devices.reshape((2,) * (bits + 1) + (fs,)), names)
    rows = lambda rank: P(names, *([None] * (rank - 1)))
    in_specs = tuple(rows(r) for r in (2, 2, 2, 2, 2, 1, 1, 1, 1, 3, 3, 2, 2, 1, 2))
    out_specs = tuple(rows(r) for r in (2, 2, 2, 2, 2, 2, 1, 1, 1, 1, 3, 3))
    return jax.shard_map(
        functools.partial(local, bits=bits, fs=fs),
        mesh=fine,
        in_specs=in_specs,
        out_specs=out_specs,
        check_vma=False,
    )
```

```python
import functools
import math

import jax
import jax.numpy as jnp
from jax import lax
from jax.experimental import pallas as pl
from jax.experimental.pallas import tpu as pltpu
from jax.sharding import Mesh
from jax.sharding import PartitionSpec as P

HEADS = 16
HEAD_DIM = 64
CAP = 640
PARTS = 2
MIB = 1 << 20

norm_eps = 1e-05
neg_large = -1e30
gelu_c = math.sqrt(2.0 / math.pi)
gelu_k = 0.044715
f32 = jnp.float32
bf16 = jnp.bfloat16


def nt_dot(a, b):
    return lax.dot_general(a, b, (((1,), (1,)), ((), ())), preferred_element_type=f32)


def tn_dot(a, b):
    return lax.dot_general(a, b, (((0,), (0,)), ((), ())), preferred_element_type=f32)


def nn_dot(a, b):
    return jnp.dot(a, b, preferred_element_type=f32)


def params(mib, steps=1):
    return pltpu.CompilerParams(
        vmem_limit_bytes=mib * MIB, dimension_semantics=("arbitrary",) * steps
    )


def cost(us):
    return pl.CostEstimate(flops=int(us * 1.15e9), bytes_accessed=MIB, transcendentals=0)


def whole(shape, buffers=None):
    zeros = (0,) * len(shape)
    if buffers is None:
        return pl.BlockSpec(shape, lambda *_: zeros)
    return pl.BlockSpec(shape, lambda *_: zeros, pipeline_mode=pl.Buffered(buffers))


def run_kernel(
    kernel, *, in_specs, inputs, out_specs, out_shape, deps=(), through=(), prefetch=None, grid=(), scratch_shapes=(), **rest
):
    first_args = [] if prefetch is None else [prefetch]
    deps, through = list(deps), list(through)
    out_specs = list(out_specs) if isinstance(out_specs, (list, tuple)) else [out_specs]
    out_shape = list(out_shape) if isinstance(out_shape, (list, tuple)) else [out_shape]
    a = len(first_args) + len(inputs)
    b = a + len(deps) + len(through)
    c = b + len(out_shape)

    def body(*refs):
        kernel(*refs[:a], *refs[b:c], *refs[c + len(through) :])

    far = pl.BlockSpec(memory_space=pl.ANY)
    spec = pltpu.PrefetchScalarGridSpec(
        num_scalar_prefetch=len(first_args),
        grid=grid,
        in_specs=list(in_specs) + [far] * (b - a),
        out_specs=out_specs + [far] * len(through),
        scratch_shapes=list(scratch_shapes),
    )
    made = pl.pallas_call(
        body,
        grid_spec=spec,
        out_shape=out_shape + [jax.ShapeDtypeStruct(t.shape, t.dtype) for t in through],
        input_output_aliases={a + len(deps) + i: len(out_shape) + i for i in range(len(through))},
        **rest,
    )(*first_args, *inputs, *deps, *through)
    return made if len(made) > 1 else made[0]


def swap(value, axis):
    return lax.ppermute(value, axis, [(0, 1), (1, 0)])


class Links:
    def __init__(self, bits, fs):
        self.bits = bits
        self.fs = fs
        self.axes = tuple(f"b{k}" for k in range(bits)) + ("core",)

    def axis(self, step, core):
        return (step + core) % self.bits

    def flip(self, step, core):
        return 1 << (self.bits - 1 - self.axis(step, core))

    def mask(self, index, core):
        return sum(self.flip(t, core) for t in range(self.bits) if index >> t & 1)

    def swap(self, value, step):
        pairs = []
        for source in range(2 << self.bits):
            core = source & 1
            pairs.append((source, source ^ (self.flip(step, core) << 1)))
        return lax.ppermute(value, self.axes, pairs)

    def gather_line(self, shard):
        spread = jnp.broadcast_to(shard[None], (self.fs,) + shard.shape)
        return lax.all_to_all(spread, "fsdp", 0, 0)

    def gather_chips(self, block):
        pieces = [block]
        for t in range(self.bits):
            pieces = pieces + [self.swap(p, t) for p in pieces]
        return pieces

    def reduce_chips(self, keep, send, steps):
        for t in reversed(range(steps)):
            got = self.swap(send, t)
            if t > 0:
                half = keep.shape[0] // 2
                send = add_low(keep[half:], got[half:])
                keep = add_low(keep[:half], got[:half])
            else:
                keep = add_low(keep[0], got[0])
        return keep

    def reduce_line_direct(self, value, zed, hold):
        total = after(pick(value, zed, 0).astype(f32), *hold)
        for t in range(1, self.fs):
            pairs = [(z, (z + t) % self.fs) for z in range(self.fs)]
            part = lax.ppermute(pick(value, (zed + t) % self.fs, 0), "fsdp", pairs)
            total = total + part.astype(f32)
        return total

    def reduce_line(self, value):
        got = lax.all_to_all(value, "fsdp", 0, 0)
        return jnp.sum(got.astype(f32), axis=0)


def add_low(a, b):
    return (a.astype(f32) + b.astype(f32)).astype(bf16)


def norm_rows(values):
    center = values - jnp.mean(values, axis=1, keepdims=True)
    inverse = lax.rsqrt(jnp.mean(center * center, axis=1, keepdims=True) + norm_eps)
    return center * inverse, inverse


def norm_back(grad_rows, scaled, inverse, gain):
    inner = grad_rows * gain
    return inverse * (
        inner
        - jnp.mean(inner, axis=1, keepdims=True)
        - scaled * jnp.mean(inner * scaled, axis=1, keepdims=True)
    )


def load_rows(ids, pieces, rows, store):
    for i, piece in enumerate(pieces):
        store(pl.multiple_of(ids[len(pieces) // 2 + i] * rows, rows), piece)


def first_kernel(ids, tok, *refs, count, rows, width):
    pieces = refs[:count]
    h_ref, qkv_ref, w_ref, g_ref, norms = refs[count:]

    @pl.when(pl.program_id(0) == 0)
    def _():
        def store(at, piece):
            w_ref[pl.ds(at, rows), :] = piece[:, width : 4 * width]
            norms[pl.ds(at, rows), :] = piece[:, 4 * width :].astype(f32)

        load_rows(ids, pieces, rows, store)
        g_ref[...] = jnp.transpose(norms[...])[:8]

    scaled, _ = norm_rows(tok[...])
    h = (scaled * g_ref[0:1, :] + g_ref[1:2, :]).astype(bf16)
    h_ref[...] = h
    for i in range(3):
        out = nn_dot(h, w_ref[:, i * width : (i + 1) * width]).astype(bf16)
        if i == 0:
            out = out * jnp.asarray(1.0 / math.sqrt(HEAD_DIM), bf16)
        qkv_ref[i] = out


def first(ids, tokens, pieces, deps):
    n, d = tokens.shape
    rows, cols = pieces[0].shape
    tile = 256
    return run_kernel(
        functools.partial(first_kernel, count=len(pieces), rows=rows, width=d),
        prefetch=ids,
        inputs=[tokens, *pieces],
        deps=deps,
        grid=(n // tile,),
        in_specs=[pl.BlockSpec((tile, d), lambda i, s: (i, 0))]
        + [whole((rows, cols), 1) for _ in pieces],
        out_specs=[
            pl.BlockSpec((tile, d), lambda i, s: (i, 0)),
            pl.BlockSpec((3, tile, d), lambda i, s: (0, i, 0)),
            whole((d, 3 * d)),
            whole((8, d)),
        ],
        scratch_shapes=[pltpu.VMEM((d, 128), f32)],
        out_shape=[
            jax.ShapeDtypeStruct((n, d), bf16),
            jax.ShapeDtypeStruct((3, n, d), bf16),
            jax.ShapeDtypeStruct((d, 3 * d), bf16),
            jax.ShapeDtypeStruct((8, d), f32),
        ],
        compiler_params=params(56),
        cost_estimate=cost(16),
        name="qkv",
    )


def make_bias(bias, kseg, qseg, n):
    key_at = lax.broadcasted_iota(jnp.int32, (256, n), 0)
    query_at = lax.broadcasted_iota(jnp.int32, (256, n), 1)
    for b in range(n // 256):
        rows = key_at + b * 256
        same = kseg[b * 256 : (b + 1) * 256, 0:1] == qseg[0:1, :]
        seen = (same & (rows <= query_at)) | (rows == query_at)
        bias[b * 256 : (b + 1) * 256, :] = jnp.where(seen, 0.0, neg_large)


def head_mask(block, head):
    lane = lax.broadcasted_iota(jnp.int32, block.shape, 1)
    return jnp.where((lane < HEAD_DIM) == (head == 0), block, jnp.zeros_like(block))


def attend_kernel(kseg, qseg, qkv, o_ref, lse_ref, bias, *, n):
    @pl.when(pl.program_id(0) == 0)
    def _():
        make_bias(bias, kseg, qseg, n)

    k = qkv[1]
    v_t = jnp.transpose(qkv[2])
    for i in range(n // 256):
        keys = (i + 1) * 256
        cols = slice(i * 256, keys)
        q = qkv[0, cols, :]
        parts = []
        for head in range(2):
            s = nt_dot(k[:keys], head_mask(q, head)) + bias[:keys, cols]
            peak = jnp.max(s, axis=0, keepdims=True)
            e = jnp.exp(s - peak)
            total = jnp.sum(e, axis=0, keepdims=True)
            p = (e * (1.0 / total)).astype(bf16)
            parts.append(nn_dot(v_t[head * HEAD_DIM : (head + 1) * HEAD_DIM, :keys], p))
            lse_ref[0, head : head + 1, cols] = peak + jnp.log(total)
        o_ref[cols, :] = jnp.transpose(jnp.concatenate(parts, axis=0)).astype(bf16)


def attend(kseg, qseg, qkv, part, parts, deps):
    _, n, d = qkv.shape
    pairs = d // 128 // parts
    d = d // parts
    return run_kernel(
        functools.partial(attend_kernel, n=n),
        inputs=[kseg, qseg, qkv],
        deps=deps,
        grid=(pairs,),
        in_specs=[
            whole(kseg.shape),
            whole(qseg.shape),
            pl.BlockSpec((3, n, 128), lambda p: (0, 0, p + part * pairs)),
        ],
        out_specs=[
            pl.BlockSpec((n, 128), lambda p: (0, p)),
            pl.BlockSpec((1, 8, n), lambda p: (p, 0, 0)),
        ],
        out_shape=[
            jax.ShapeDtypeStruct((n, d), bf16),
            jax.ShapeDtypeStruct((pairs, 8, n), f32),
        ],
        scratch_shapes=[pltpu.VMEM((n, n), f32)],
        compiler_params=params(48),
        cost_estimate=cost(21),
        name="attend",
    )


def attend_back_kernel(kseg, qseg, qkv, do_ref, lse_ref, out, bias, dk_acc, dv_acc, *, n):
    @pl.when(pl.program_id(0) == 0)
    def _():
        make_bias(bias, kseg, qseg, n)

    k = qkv[1]
    v = qkv[2]
    k_t = jnp.transpose(k)
    blocks = n // 256
    for i in reversed(range(blocks)):
        keys = (i + 1) * 256
        cols = slice(i * 256, keys)
        parts = []
        for head in range(2):
            q = head_mask(qkv[0, cols, :], head)
            go = head_mask(do_ref[cols, :], head)
            s = nt_dot(k[:keys], q) + bias[:keys, cols]
            p = jnp.exp(s - lse_ref[0, head : head + 1, cols])
            dp = nt_dot(v[:keys], go)
            inner = jnp.sum(p * dp, axis=0, keepdims=True)
            ds = (p * (dp - inner)).astype(bf16)
            dv = nn_dot(p.astype(bf16), go)
            dk = nn_dot(ds, q)
            if i == blocks - 1 and head == 0:
                dv_acc[...] = dv
                dk_acc[...] = dk
            else:
                dv_acc[:keys, :] += dv
                dk_acc[:keys, :] += dk
            parts.append(nn_dot(k_t[head * HEAD_DIM : (head + 1) * HEAD_DIM, :keys], ds))
        dq = jnp.concatenate(parts, axis=0) * (1.0 / math.sqrt(HEAD_DIM))
        out[0, cols, :] = jnp.transpose(dq).astype(bf16)
    out[1] = dk_acc[...].astype(bf16)
    out[2] = dv_acc[...].astype(bf16)


def attend_back(kseg, qseg, qkv, grad_mixed, lse, part, parts, deps):
    _, n, d = qkv.shape
    pairs = d // 128 // parts
    d = d // parts
    return run_kernel(
        functools.partial(attend_back_kernel, n=n),
        inputs=[kseg, qseg, qkv, grad_mixed, lse],
        deps=deps,
        grid=(pairs,),
        in_specs=[
            whole(kseg.shape),
            whole(qseg.shape),
            pl.BlockSpec((3, n, 128), lambda p: (0, 0, p + part * pairs)),
            pl.BlockSpec((n, 128), lambda p: (0, p + part * pairs)),
            pl.BlockSpec((1, 8, n), lambda p: (p, 0, 0)),
        ],
        out_specs=pl.BlockSpec((3, n, 128), lambda p: (0, 0, p)),
        out_shape=jax.ShapeDtypeStruct((3, n, d), bf16),
        scratch_shapes=[
            pltpu.VMEM((n, n), f32),
            pltpu.VMEM((n, 128), f32),
            pltpu.VMEM((n, 128), f32),
        ],
        compiler_params=params(56),
        cost_estimate=cost(22),
        name="attend_back",
    )


def slot_hot(slot_row, start, count):
    n = slot_row.shape[1]
    at = lax.broadcasted_iota(jnp.int32, (count, n), 0) + start
    return jnp.where(at == slot_row, 1.0, 0.0).astype(bf16)


def pack_kernel(slot_row, values, own, other):
    low = values[...].astype(bf16)
    own[...] = nn_dot(slot_hot(slot_row[0:1, :], 0, CAP), low).astype(bf16)
    other[...] = nn_dot(slot_hot(slot_row[0:1, :], CAP, CAP), low).astype(bf16)


def pack(slot_row, values, deps):
    n, d = values.shape
    return run_kernel(
        pack_kernel,
        inputs=[slot_row, values],
        deps=deps,
        in_specs=[whole(slot_row.shape), whole((n, d))],
        out_specs=[whole((CAP, d))] * 2,
        out_shape=[jax.ShapeDtypeStruct((CAP, d), bf16)] * 2,
        compiler_params=pltpu.CompilerParams(vmem_limit_bytes=48 * MIB),
        cost_estimate=cost(0.1),
        name="pack",
    )


def second_kernel(ids, slot_row, tok, gains, *refs, count, rows, steps, tile, parts):
    mixed, refs = refs[:parts], refs[parts:]
    pieces = refs[:count]
    x_ref, w_ref, own, other, h_all = refs[count:]
    step = pl.program_id(0)

    @pl.when(step == 0)
    def _():
        def store(at, piece):
            w_ref[pl.ds(at, rows), :] = piece[...]

        load_rows(ids, pieces, rows, store)

    x = tok[...]
    wide = mixed[0].shape[1]
    for i, o_ref in enumerate(mixed):
        x = x + nn_dot(o_ref[...], w_ref[i * wide : (i + 1) * wide, :])
    x_ref[...] = x
    scaled, _ = norm_rows(x)
    h = (scaled * gains[2:3, :] + gains[3:4, :]).astype(bf16)
    h_all[pl.ds(pl.multiple_of(step * tile, tile), tile), :] = h

    @pl.when(step == steps - 1)
    def _():
        own[...] = nn_dot(slot_hot(slot_row[0:1, :], 0, CAP), h_all[...]).astype(bf16)
        other[...] = nn_dot(slot_hot(slot_row[0:1, :], CAP, CAP), h_all[...]).astype(bf16)


def second(ids, slot_row, mixed, tokens, gains, pieces, deps):
    n, d = tokens.shape
    rows = pieces[0].shape[0]
    tile = 256
    return run_kernel(
        functools.partial(
            second_kernel, count=len(pieces), rows=rows, steps=n // tile, tile=tile, parts=len(mixed)
        ),
        prefetch=ids,
        inputs=[slot_row, tokens, gains, *mixed, *pieces],
        deps=deps,
        **dict(
            grid=(n // tile,),
            in_specs=[
                whole(slot_row.shape),
                pl.BlockSpec((tile, d), lambda i, s: (i, 0)),
                whole(gains.shape),
            ]
            + [pl.BlockSpec((tile, o.shape[1]), lambda i, s: (i, 0)) for o in mixed]
            + [whole((rows, d), 1) for _ in pieces],
            out_specs=[
                pl.BlockSpec((tile, d), lambda i, s: (i, 0)),
                whole((d, d)),
                whole((CAP, d)),
                whole((CAP, d)),
            ],
            scratch_shapes=[pltpu.VMEM((n, d), bf16)],
        ),
        out_shape=[
            jax.ShapeDtypeStruct((n, d), f32),
            jax.ShapeDtypeStruct((d, d), bf16),
            jax.ShapeDtypeStruct((CAP, d), bf16),
            jax.ShapeDtypeStruct((CAP, d), bf16),
        ],
        compiler_params=params(56),
        cost_estimate=cost(1),
        name="mix_out",
    )


def expert_kernel(ids, *refs, count, rows, tile, first_chunk, block):
    xs, ys = refs[0:2], refs[2:4]
    pos = 4
    prior = None
    if not first_chunk:
        prior = refs[pos : pos + 2]
        pos += 2
    pieces = refs[pos : pos + count]
    pos += count
    near, far, keep, send = refs[pos : pos + 4]
    x_s, dy_s, win_s, wout_s, y_acc, h_acc, a_s, du_s, sems = refs[pos + 4 :]
    half = count // 2
    step = pl.program_id(0)
    d = x_s.shape[1]
    slabs = win_s.shape[1] // d
    total = 2 * CAP

    @pl.when(step == 0)
    def _():
        copies = []

        def fetch(source, target):
            copy = pltpu.make_async_copy(source, target, sems.at[len(copies)])
            copy.start()
            copies.append(copy)

        for side in range(2):
            fetch(xs[side], x_s.at[pl.ds(side * CAP, CAP)])
        for i in range(count):
            at = pl.multiple_of(ids[i] * rows, rows)
            for h in range(slabs):
                fetch(
                    pieces[i].at[pl.ds(h * rows, rows)],
                    win_s.at[pl.ds(at, rows), pl.ds(h * d, d)],
                )
        for side in range(2):
            fetch(ys[side], dy_s.at[pl.ds(side * CAP, CAP)])
        for i in range(count):
            at = pl.multiple_of(ids[i] * tile, tile)
            fetch(pieces[i].at[pl.ds(slabs * rows, tile)], wout_s.at[pl.ds(at, tile)])
        if first_chunk:
            y_acc[...] = jnp.zeros_like(y_acc)
            h_acc[...] = jnp.zeros_like(h_acc)
        else:
            for side in range(2):
                span = slice(side * CAP, (side + 1) * CAP)
                y_acc[span, :] = prior[side][0].astype(f32)
                h_acc[span, :] = prior[side][1].astype(f32)
        for copy in copies:
            copy.wait()

    at = pl.multiple_of(ids[step] * tile, tile)

    def one_block(b, carry):
        span = pl.ds(pl.multiple_of(b * block, block), block)
        u = nn_dot(x_s[span, :], win_s[:, pl.ds(at, tile)])
        da = nt_dot(dy_s[span, :], wout_s[pl.ds(at, tile), :])
        square = u * u
        t = jnp.tanh(gelu_c * (u * (1.0 + gelu_k * square)))
        up = 0.5 * (1.0 + t)
        slope = up + (0.5 * gelu_c) * u * (1.0 - t * t) * (1.0 + 3.0 * gelu_k * square)
        a = (u * up).astype(bf16)
        du = (da * slope).astype(bf16)
        a_s[span, :] = a
        du_s[span, :] = du
        y_acc[span, :] += nn_dot(a, wout_s[pl.ds(at, tile), :])
        h_acc[span, :] += nt_dot(du, win_s[:, pl.ds(at, tile)])
        return carry

    lax.fori_loop(0, total // block, one_block, 0, unroll=True)
    grad = tn_dot(a_s[...], dy_s[...]).astype(bf16)

    for i in range(count):

        @pl.when(step == i)
        def _():
            (keep if i < half else send)[i % half, slabs * rows :, :] = grad

    slab = at // d
    row = pl.multiple_of(slab * rows, rows)
    col = pl.multiple_of(at - slab * d, tile)

    for i in range(count):
        src = pl.multiple_of(ids[i] * rows, rows)
        (keep if i < half else send)[i % half, pl.ds(row, rows), pl.ds(col, tile)] = tn_dot(
            x_s[:, pl.ds(src, rows)], du_s[...]
        ).astype(bf16)

    @pl.when(step == count - 1)
    def _():
        for side in range(2):
            span = slice(side * CAP, (side + 1) * CAP)
            (near, far)[side][0] = y_acc[span, :].astype(bf16)
            (near, far)[side][1] = h_acc[span, :].astype(bf16)


def expert(ids, xs, ys, prior, pieces, rows, tile, deps):
    count = len(pieces)
    d = xs[0].shape[1]
    hc = count * tile
    total = 2 * CAP
    first_chunk = prior is None
    far = pl.BlockSpec(memory_space=pl.ANY)
    part = (count // 2,) + pieces[0].shape
    return run_kernel(
        functools.partial(
            expert_kernel, count=count, rows=rows, tile=tile, first_chunk=first_chunk, block=320
        ),
        prefetch=ids,
        inputs=list(xs) + list(ys) + list(prior or ()) + list(pieces),
        deps=deps,
        grid=(count,),
        in_specs=[far] * 4
        + ([] if first_chunk else [whole((2, CAP, d), 1)] * 2)
        + [far] * count,
        out_specs=[whole((2, CAP, d), 1)] * 2 + [whole(part, 1)] * 2,
        scratch_shapes=[
            pltpu.VMEM((total, d), bf16),
            pltpu.VMEM((total, d), bf16),
            pltpu.VMEM((d, hc), bf16),
            pltpu.VMEM((hc, d), bf16),
            pltpu.VMEM((total, d), f32),
            pltpu.VMEM((total, d), f32),
            pltpu.VMEM((total, tile), bf16),
            pltpu.VMEM((total, tile), bf16),
            pltpu.SemaphoreType.DMA((4 + (hc // d + 1) * count,)),
        ],
        out_shape=[jax.ShapeDtypeStruct((2, CAP, d), bf16)] * 2
        + [jax.ShapeDtypeStruct(part, bf16)] * 2,
        compiler_params=params(60),
        cost_estimate=cost(53),
        name="experts",
    )


def third_kernel(slot_col, gains, x_ref, cot, w_ref, *refs):
    near, far, out_ref, mid_ref, dz_ref, do_ref, g_ref = refs
    tile = x_ref.shape[0]
    at = lax.broadcasted_iota(jnp.int32, (tile, CAP), 1)
    own = jnp.where(slot_col[:, 0:1] == at, 1.0, 0.0).astype(bf16)
    other = jnp.where(slot_col[:, 0:1] == at + CAP, 1.0, 0.0).astype(bf16)
    x = x_ref[...]
    out_ref[...] = x + nn_dot(own, near[0]) + nn_dot(other, far[0])
    dh = nn_dot(own, near[1]) + nn_dot(other, far[1])
    scaled, inverse = norm_rows(x)
    mid = cot[...] + norm_back(dh, scaled, inverse, gains[2:3, :])
    mid_ref[...] = mid
    dz = mid.astype(bf16)
    dz_ref[...] = dz
    do_ref[...] = nt_dot(dz, w_ref[...]).astype(bf16)

    @pl.when(pl.program_id(0) == 0)
    def _():
        g_ref[...] = jnp.zeros_like(g_ref)

    g_ref[0:1, :] += jnp.sum(dh * scaled, axis=0, keepdims=True)
    g_ref[1:2, :] += jnp.sum(dh, axis=0, keepdims=True)


def third(slot_col, gains, middle, cot, w_out, returned, deps, through):
    n, d = middle.shape
    tile = 256
    row = pl.BlockSpec((tile, d), lambda i: (i, 0))
    return run_kernel(
        third_kernel,
        inputs=[slot_col, gains, middle, cot, w_out, *returned],
        deps=deps,
        through=through,
        grid=(n // tile,),
        in_specs=[
            pl.BlockSpec((tile, slot_col.shape[1]), lambda i: (i, 0)),
            whole(gains.shape),
            row,
            row,
            whole((d, d), 1),
        ]
        + [whole((2, CAP, d), 1)] * 2,
        out_specs=[row, row, row, row, whole((8, d))],
        out_shape=[
            jax.ShapeDtypeStruct((n, d), f32),
            jax.ShapeDtypeStruct((n, d), f32),
            jax.ShapeDtypeStruct((n, d), bf16),
            jax.ShapeDtypeStruct((n, d), bf16),
            jax.ShapeDtypeStruct((8, d), f32),
        ],
        compiler_params=params(56),
        cost_estimate=cost(17),
        name="combine",
    )


def weights_kernel(ids, *refs, count, rows, groups, steps):
    total = sum(groups)
    lefts, rights = refs[:total], refs[total : total + len(groups)]
    keep, send, res, *turned = refs[total + len(groups) :]
    step = pl.program_id(0)

    @pl.when(step == 0)
    def _():
        k = 0
        for size, left_t in zip(groups, turned):
            wide = lefts[k].shape[1]
            for i in range(size):
                left_t[i * wide : (i + 1) * wide, :] = jnp.transpose(lefts[k + i][...])
            k += size

    start = 0
    for right, left_t, size in zip(rights, turned, steps):

        @pl.when((step >= start) & (step < start + size))
        def _():
            res[...] = nn_dot(left_t[...], right[0])

        start += size
    for i in range(count):
        for out, r in ((keep, count + i), (send, 2 * count + i)):
            src = pl.multiple_of(ids[r] * rows, rows)
            out[i] = res[pl.ds(src, rows), :].astype(bf16)


def weights(ids, products, count, us, deps=(), tile=512):
    n = products[0][1].shape[1]
    d = sum(left.shape[1] for left in products[0][0])
    rows = d // (2 * count)
    steps = [right.shape[0] * right.shape[2] // tile for _, right in products]
    in_specs = [whole(left.shape, 1) for lefts, _ in products for left in lefts]
    start = 0
    for (_, right), size in zip(products, steps):
        per = right.shape[2] // tile

        def place(j, s, start=start, size=size, per=per):
            at = jnp.clip(j - start, 0, size - 1)
            return at // per, 0, at % per

        in_specs.append(pl.BlockSpec((1, n, tile), place))
        start += size
    out = pl.BlockSpec((count, rows, tile), lambda j, s: (0, 0, j))
    return run_kernel(
        functools.partial(
            weights_kernel,
            count=count,
            rows=rows,
            groups=[len(lefts) for lefts, _ in products],
            steps=steps,
        ),
        prefetch=ids,
        inputs=[left for lefts, _ in products for left in lefts] + [right for _, right in products],
        deps=deps,
        grid=(start,),
        in_specs=in_specs,
        out_specs=[out, out],
        scratch_shapes=[pltpu.VMEM((d, tile), f32)] + [pltpu.VMEM((d, n), bf16) for _ in products],
        out_shape=[jax.ShapeDtypeStruct((count, rows, start * tile), bf16)] * 2,
        compiler_params=params(48),
        cost_estimate=cost(us),
        name="weight_grads",
    )


def last_kernel(gains, tok, mid, w_ref, *refs):
    grads, (out_ref, g_ref) = refs[:-2], refs[-2:]
    d = tok.shape[1]
    wide = grads[0].shape[2]
    dh = None
    for j, grad in enumerate(grads):
        for i in range(3):
            at = i * d + j * wide
            term = nt_dot(grad[i], w_ref[:, at : at + wide])
            dh = term if dh is None else dh + term
    scaled, inverse = norm_rows(tok[...])
    out_ref[...] = mid[...] + norm_back(dh, scaled, inverse, gains[0:1, :])

    @pl.when(pl.program_id(0) == 0)
    def _():
        g_ref[...] = jnp.zeros_like(g_ref)

    g_ref[0:1, :] += jnp.sum(dh * scaled, axis=0, keepdims=True)
    g_ref[1:2, :] += jnp.sum(dh, axis=0, keepdims=True)


def last(gains, tokens, middle_grad, dqkv, w_qkv, deps):
    n, d = tokens.shape
    tile = 256
    row = pl.BlockSpec((tile, d), lambda i: (i, 0))
    return run_kernel(
        last_kernel,
        inputs=[gains, tokens, middle_grad, w_qkv, *dqkv],
        deps=deps,
        grid=(n // tile,),
        in_specs=[
            whole(gains.shape),
            row,
            row,
            whole((d, 3 * d), 1),
        ]
        + [pl.BlockSpec((3, tile, g.shape[2]), lambda i: (0, i, 0)) for g in dqkv],
        out_specs=[row, whole((8, d))],
        out_shape=[jax.ShapeDtypeStruct((n, d), f32), jax.ShapeDtypeStruct((8, d), f32)],
        compiler_params=params(48),
        cost_estimate=cost(1),
        name="token_grads",
    )


def pick(value, index, axis):
    return lax.dynamic_index_in_dim(value, index, axis, keepdims=False)


def after(value, *others):
    for other in others:
        mark = lax.slice(other, (0,) * other.ndim, (1,) * other.ndim).reshape(()) * jnp.zeros((), other.dtype)
        value = value + mark.astype(value.dtype)
    return value


def in_order(core, mine, theirs):
    return jnp.where(core == 0, jnp.stack([mine, theirs]), jnp.stack([theirs, mine]))


def local(
    tokens,
    w_query,
    w_key,
    w_value,
    w_output,
    gain_one,
    shift_one,
    gain_two,
    shift_two,
    expert_in,
    expert_out,
    lengths,
    expert_ids,
    padding,
    cotangent,
    *,
    bits,
    fs,
):
    n, d = tokens.shape
    share, _, hidden = expert_in.shape
    owned = expert_out.shape[0]
    chips = 1 << bits
    devices = 2 * chips * fs
    hc = hidden // 2
    links = Links(bits, fs)
    core = lax.axis_index("core")
    zed = lax.axis_index("fsdp")
    chip = jnp.int32(0)
    for k in range(bits):
        chip = chip * 2 + lax.axis_index(f"b{k}")
    orders = jnp.array([[links.mask(i, c) for i in range(chips)] for c in range(2)], jnp.int32)
    near, far = chip ^ pick(orders, core, 0), chip ^ pick(orders, 1 - core, 0)
    ids = jnp.concatenate([near, near * 2 + core, far * 2 + 1 - core]).astype(jnp.int32)

    norms = jnp.stack([gain_one, shift_one, gain_two, shift_two], axis=1)
    norms = jnp.pad(norms, ((0, 0), (0, 124)))
    shard = jnp.concatenate([w_output, w_query, w_key, w_value, norms], axis=1).astype(bf16)
    line = links.gather_line(shard).reshape(fs * share, -1)

    def gather_attention(block):
        own = links.gather_chips(block)
        return own + [swap(piece, "core") for piece in own]

    pieces = gather_attention(line)

    slabs = hc // d
    in_rows, out_rows = 2 * fs * share, fs * owned
    in_low = expert_in.astype(bf16).reshape(share, 2, chips, 2, fs * owned).transpose(1, 3, 0, 2, 4)
    in_low = in_low.reshape(2, 2, share, slabs, d).transpose(0, 1, 3, 2, 4).reshape(2, -1, d)
    low = jnp.concatenate([in_low, expert_out.astype(bf16).transpose(1, 0, 2)], axis=1)
    pair = in_order(core, pick(low, core, 0), swap(pick(low, 1 - core, 0), "core"))
    in_pair = pair[:, : 2 * slabs * share].reshape(2, 2, slabs * share, d)
    out_pair = pair[:, 2 * slabs * share :]

    def gather_experts(j, before, gate):
        mine = jnp.concatenate([in_pair[:, j].reshape(-1, d), out_pair[j]], axis=0)
        got = after(links.gather_line(after(mine, before)), gate)
        in_part = got[:, : 2 * slabs * share].reshape(fs, 2, slabs, share, d)
        in_part = in_part.transpose(2, 1, 0, 3, 4).reshape(slabs * in_rows, d)
        out_part = got[:, 2 * slabs * share :].reshape(out_rows, d)
        return jnp.concatenate([in_part, out_part], axis=0)

    spots = jnp.arange(n, dtype=jnp.int32)
    eight = jnp.arange(lengths.shape[1])
    ends = jnp.sum(jnp.where(eight[:, None] <= eight[None, :], lengths[0][:, None], 0), axis=0)
    segment = jnp.sum((spots[:, None] >= ends[None, :]).astype(jnp.int32), axis=1)
    key_segment = jnp.where(padding == 1, segment, -1)
    kseg = jnp.broadcast_to(key_segment[:, None], (n, 128))
    qseg = jnp.broadcast_to(segment[None, :], (8, n))
    chosen = expert_ids[:, 0]
    names = jnp.arange(2, dtype=jnp.int32)
    hot = (chosen[:, None] == names[None, :]).astype(bf16)
    before = (spots[:, None] > spots[None, :]).astype(bf16)
    place = nn_dot(before, hot).astype(jnp.int32)
    place = jnp.where(chosen == 0, place[:, 0], place[:, 1])
    slot = jnp.where(chosen == core, place, CAP + place)
    slot_row = jnp.broadcast_to(slot[None, :], (8, n))
    slot_col = jnp.broadcast_to(slot[:, None], (n, 128))

    lines = [gather_experts(0, line, pieces[1])]
    h1, qkv, w_qkv, gains = first(ids, tokens, pieces, lines[:1])

    dy_own, dy_other = pack(slot_row, cotangent, [h1])
    dys = (dy_own, swap(dy_other, "core"))

    def spread_chunk(block, hold):
        pieces = [block]
        for t in range(bits):
            if t == bits - 1:
                pieces = [after(block, pieces[-1] if hold is None else hold)] + pieces[1:]
            pieces = pieces + [links.swap(p, t) for p in pieces]
        return [block] + pieces[1:]

    chunks = [spread_chunk(lines[0], h1)]
    lines.append(gather_experts(1, lines[0], h1))
    mixed, lse = [], []
    for i in range(PARTS):
        needs = [*lse[-1:], *chunks[0][2:-1], lines[1]] if i else [chunks[0][1]]
        made = attend(kseg, qseg, qkv, i, PARTS, needs)
        mixed.append(made[0])
        lse.append(made[1])
    chunks.append(spread_chunk(lines[1], None))
    middle, w_out, x_own, x_other = second(
        ids, slot_row, mixed, tokens, gains, pieces, []
    )
    xs = (x_own, swap(x_other, "core"))

    def line_rows(total):
        in_part = total[: slabs * in_rows].reshape(slabs, 2, fs, share, d)
        in_part = in_part.transpose(2, 1, 0, 3, 4).reshape(fs, 2 * slabs * share, d)
        return jnp.concatenate([in_part, total[slabs * in_rows :].reshape(fs, owned, d)], axis=1)

    def chip_sum(keep, send, gate):
        got = links.swap(send, bits - 1)
        for t in reversed(range(bits - 1)):
            top = keep.shape[0] // 2
            send = add_low(keep[top:], got[top:])
            total = keep[:top].astype(f32) + got[:top].astype(f32)
            first_send.append(send)
            got = links.swap(send, t)
            if t:
                keep = total.astype(bf16)
            else:
                return after((total + got.astype(f32)).astype(bf16)[0], *gate)
        return after(add_low(keep[0], got[0]), *gate)

    half = chips // 2
    near, far, keep_a, send_a = expert(ids, xs, dys, None, chunks[0], in_rows, out_rows, [chunks[1][1]])
    near, far, keep_b, send_b = expert(ids, xs, dys, [near, far], chunks[1], in_rows, out_rows, [])
    returned = (near, swap(far, "core"))

    first_send = []
    chunk_a = chip_sum(keep_a, send_a, [])
    output, grad_middle, dz, grad_mixed, sums_two, send_b = third(
        slot_col, gains, middle, cotangent, w_out, returned, first_send, [send_b]
    )

    def core_sum(made):
        return add_low(made[0], swap(made[1], "core"))

    def split_sum(total):
        got = links.swap(total[half:], bits - 1)
        return add_low(total[:half], got)

    def rest_sum(total):
        if bits > 1:
            top = total.shape[0] // 2
            total = links.reduce_chips(total[:top], total[top:], bits - 1)
        else:
            total = total[0]
        return total.reshape(fs, share, -1)

    wide = d // PARTS
    chunk_a = line_rows(after(chunk_a, dz))
    line_a = links.reduce_line(chunk_a)
    grads = [attend_back(kseg, qseg, qkv, grad_mixed, lse[0], 0, PARTS, [chunk_a])]
    made_a = weights(ids, [(mixed, dz[None]), ([h1], grads[0])], chips, 0.1)
    first_send = []
    chunk_b = chip_sum(keep_b, send_b, [])
    grads.append(
        attend_back(kseg, qseg, qkv, grad_mixed, lse[1], 1, PARTS, [made_a[1], *first_send])
    )
    chunk_b = line_rows(after(chunk_b, grads[1]))
    line_b = links.reduce_line(chunk_b)
    core_a = after(core_sum(made_a), grads[1])
    made_b = weights(ids, [([h1], grads[1])], chips, 0.1, [core_a, chunk_b])
    core_b = core_sum(made_b)
    split_a, split_b = split_sum(core_a), after(split_sum(core_b), line_b)
    ready = [rest_sum(split_a), rest_sum(split_b)]
    grad_tokens, sums_one = last(gains, tokens, grad_middle, grads, w_qkv, [core_b])
    ins = jnp.stack([t[: 2 * slabs * share].reshape(2, slabs * share, d) for t in (line_a, line_b)])
    outs = jnp.stack([t[2 * slabs * share :] for t in (line_a, line_b)])
    theirs = jnp.concatenate([pick(ins, 1 - core, 1).reshape(-1, d), pick(outs, 1 - core, 0)], axis=0)
    got = swap(theirs, "core")
    in_grad = in_order(core, pick(ins, core, 1).reshape(-1, d), got[: 2 * slabs * share])
    in_grad = in_grad.reshape(2, 2, slabs, share, d // (fs * owned), fs * owned)
    grad_expert_in = in_grad.transpose(3, 0, 2, 4, 1, 5).reshape(share, 2, hidden)
    out_grad = in_order(core, pick(outs, core, 0), got[2 * slabs * share :])
    grad_expert_out = out_grad.transpose(1, 0, 2)

    ready = links.reduce_line_direct(jnp.concatenate(ready, axis=2), zed, [grad_expert_in, grad_expert_out])
    grad_output = ready[:, :d]
    grad_qkv = [
        jnp.concatenate(
            [ready[:, d + (3 * j + i) * wide : d + (3 * j + i + 1) * wide] for j in range(PARTS)],
            axis=1,
        )
        for i in range(3)
    ]

    sums = jnp.concatenate([sums_one[:2], sums_two[:2]]).reshape(4, devices, share).transpose(1, 0, 2)
    sums = after(sums, line_b)
    sums = jnp.sum(lax.all_to_all(sums, links.axes + ("fsdp",), 0, 0), axis=0)

    return (
        output,
        grad_tokens,
        grad_qkv[0],
        grad_qkv[1],
        grad_qkv[2],
        grad_output,
        sums[0],
        sums[1],
        sums[2],
        sums[3],
        grad_expert_in,
        grad_expert_out,
    )


def solution(mesh):
    dp, fs = mesh.shape["dp"], mesh.shape["fsdp"]
    bits = (dp // 2).bit_length() - 1
    names = tuple(f"b{k}" for k in range(bits)) + ("core", "fsdp")
    fine = Mesh(mesh.devices.reshape((2,) * (bits + 1) + (fs,)), names)
    rows = lambda rank: P(names, *([None] * (rank - 1)))
    in_specs = tuple(rows(r) for r in (2, 2, 2, 2, 2, 1, 1, 1, 1, 3, 3, 2, 2, 1, 2))
    out_specs = tuple(rows(r) for r in (2, 2, 2, 2, 2, 2, 1, 1, 1, 1, 3, 3))
    return jax.shard_map(
        functools.partial(local, bits=bits, fs=fs),
        mesh=fine,
        in_specs=in_specs,
        out_specs=out_specs,
        check_vma=False,
    )
```
